128 devices in a mesh: scan: 32 (over y, x, core), cuts: 4 (over z).
Axes of the slice: x: 4, y: 4, z: 4, core: 2. Of those that a mesh axis runs over, the one named last changes fastest.
Arguments:
- probe_wave: bfloat16 [2, 512, 512], replicated, may hold values from -6 to 6
- propagator: bfloat16 [2, 512, 512], replicated
- object_slices: float32 [2, 4, 4096, 2048], P(None, 'cuts', 'scan'), may hold values from -4 to 4
- positions: int32 [64, 2], P('scan'), may hold values from 0 to 4095, as said below
- intensities: float32 [64, 512, 512], P('scan'), may hold values from 0 to 2
Outputs:
- object_gradient: float32 [2, 4, 4096, 2048], P(None, 'cuts', 'scan')
The draws below stay inside these ranges and needn't reach their ends.
Inputs may be any that keep to these rules, and one draw needn't show every extreme that they name: `positions`: position j's row lies in [128 * (j // 2), 128 * (j // 2 + 1)); on every index of scan some position's row is the last of that range. Columns lie in 0 to 1536, both ends reached.
All inputs are finite; a program needn't handle non-finite values.
Results may differ from the reference program's by a relative error of at most 0.019.
Values may be sent and summed in bfloat16 or wider, within the bound.
A program may use at most 128 MiB of HBM per device.

```python
import math
import jax
import jax.numpy as jnp
from jax import lax

P_SIZE = 512
BAND = 128
OW = 2048
POS_DEV = 2
NSL = 4
OH = 4096
NPOS = 64


def draw_propagator(key, part):
    scatter_part = jax.random.normal(key, (2, P_SIZE, P_SIZE), jnp.float32) * (0.3 / P_SIZE ** 0.5)
    identity_part = jnp.eye(P_SIZE, dtype=jnp.float32) * 0.8
    return (scatter_part + jnp.stack([identity_part, jnp.zeros_like(identity_part)])).astype(jnp.bfloat16)


def draw_positions(key, part):
    row_key, column_key = jax.random.split(key)
    serial = jnp.arange(NPOS, dtype=jnp.int32)
    device = serial // POS_DEV
    offset = jax.random.randint(row_key, (NPOS,), 0, BAND, dtype=jnp.int32)
    offset = jnp.where(serial % POS_DEV == device % POS_DEV, BAND - 1, offset)
    column = jax.random.randint(column_key, (NPOS,), 0, OW - P_SIZE + 1, dtype=jnp.int32)
    column = jnp.where(serial == 0, OW - P_SIZE, column)
    column = jnp.where(serial == 1, 0, column)
    return jnp.stack([device * BAND + offset, column], axis=1).astype(jnp.int32)


def shard_levels(key, extent, cuts, smallest, largest):
    factor_of = 1.0
    for dim, shards_of in cuts:
        heights = jax.random.uniform(jax.random.fold_in(jax.random.fold_in(key, 6), dim), (shards_of,), jnp.float32, smallest / len(cuts), largest / len(cuts))
        factor_of = factor_of * jnp.repeat(jnp.exp(heights), extent[dim] // shards_of).reshape((-1,) + (1,) * (len(extent) - 1 - dim))
    return factor_of


def gaussian(own_key, shape, scale, bound, cuts=(), held_as=jnp.bfloat16):
    drawn = scale * jax.random.normal(own_key, shape, jnp.float32)
    if cuts:
        drawn = drawn * shard_levels(own_key, shape, cuts, -0.22, 0.18)
    return jnp.clip(drawn, -bound, bound).astype(held_as)


def setup_inputs(seed: int = 0) -> dict:
    key_of = jax.random.split(jax.random.key(seed), 6)
    probe_wave = gaussian(key_of[0], (2, P_SIZE, P_SIZE), 1.0, 6.0)
    propagator = draw_propagator(jax.random.fold_in(key_of[5], 71), 0)
    object_slices = gaussian(key_of[2], (2, NSL, OH, OW), 0.7, 4.0, ((1, 4), (2, 32)), jnp.float32)
    positions = draw_positions(jax.random.fold_in(key_of[5], 71), 0)
    intensities = jnp.clip(2.0 * jax.random.uniform(key_of[4], (NPOS, P_SIZE, P_SIZE), jnp.float32) ** shard_levels(key_of[4], (NPOS, P_SIZE, P_SIZE), ((0, 32),), -0.2, 0.2), 0.0, 2.0)
    return dict(probe_wave=probe_wave, propagator=propagator, object_slices=object_slices, positions=positions, intensities=intensities)


def complex_product(left_re, left_im, right_re, right_im):
    real_part = jnp.dot(left_re, right_re, preferred_element_type=jnp.float32) - jnp.dot(left_im, right_im, preferred_element_type=jnp.float32)
    imag_part = jnp.dot(left_re, right_im, preferred_element_type=jnp.float32) + jnp.dot(left_im, right_re, preferred_element_type=jnp.float32)
    return jnp.stack([real_part, imag_part])

def dft_table(length):
    serial = jnp.arange(length, dtype=jnp.int32)
    angle_index = serial[:, None] * serial[None, :] % length
    phase_angle = angle_index.astype(jnp.float32) * (2.0 * math.pi / length)
    norm_scale = 1.0 / math.sqrt(length)
    return jnp.stack([jnp.cos(phase_angle) * norm_scale, -jnp.sin(phase_angle) * norm_scale]).astype(jnp.bfloat16)

def forward_section(wave_in, window, propagator):
    mixed_re = wave_in[0] * window[0] - wave_in[1] * window[1]
    mixed_im = wave_in[0] * window[1] + wave_in[1] * window[0]
    mixed = jnp.stack([mixed_re, mixed_im]).astype(jnp.bfloat16)
    halfway = complex_product(propagator[0], propagator[1], mixed[0], mixed[1]).astype(jnp.bfloat16)
    return complex_product(halfway[0], halfway[1], propagator[0].T, propagator[1].T).astype(jnp.bfloat16)

def far_gradient(exit_wave, measured, transform):
    spread = complex_product(transform[0], transform[1], exit_wave[0], exit_wave[1]).astype(jnp.bfloat16)
    farfield = complex_product(spread[0], spread[1], transform[0], transform[1])
    excess = farfield[0] * farfield[0] + farfield[1] * farfield[1] - measured
    residue = (excess[None] * farfield).astype(jnp.bfloat16)
    inverse_im = -transform[1]
    pulled = complex_product(transform[0], inverse_im, residue[0], residue[1]).astype(jnp.bfloat16)
    return complex_product(pulled[0], pulled[1], transform[0], inverse_im).astype(jnp.bfloat16)

def adjoint_section(grad_out, wave_in, window, propagator):
    conj_im = -propagator[1]
    grad_half = complex_product(grad_out[0], grad_out[1], propagator[0], conj_im).astype(jnp.bfloat16)
    grad_mixed = complex_product(propagator[0].T, conj_im.T, grad_half[0], grad_half[1])
    object_re = wave_in[0] * grad_mixed[0] + wave_in[1] * grad_mixed[1]
    object_im = wave_in[0] * grad_mixed[1] - wave_in[1] * grad_mixed[0]
    wave_re = window[0] * grad_mixed[0] + window[1] * grad_mixed[1]
    wave_im = window[0] * grad_mixed[1] - window[1] * grad_mixed[0]
    return (jnp.stack([object_re, object_im]), jnp.stack([wave_re, wave_im]).astype(jnp.bfloat16))

def reference(probe_wave, propagator, object_slices, positions, intensities):
    window_size = probe_wave.shape[1]
    slices = object_slices.shape[1]
    height = object_slices.shape[2]
    width = object_slices.shape[3]
    widened = jnp.concatenate([object_slices, object_slices[:, :, :window_size]], axis=2)
    transform = dft_table(window_size)

    def one_position(gradient_sum, inputs):
        position, measured = inputs
        corner = (jnp.int32(0), jnp.int32(0), position[0].astype(jnp.int32), position[1].astype(jnp.int32))
        windows = lax.dynamic_slice(widened, corner, (2, slices, window_size, window_size))
        waves = []
        wave_now = probe_wave
        for slice_index in range(slices):
            waves.append(wave_now)
            wave_now = forward_section(wave_now, windows[:, slice_index], propagator)
        grad_wave = far_gradient(wave_now, measured, transform)
        object_grads = [None] * slices
        for slice_index in range(slices - 1, -1, -1):
            object_grads[slice_index], grad_wave = adjoint_section(grad_wave, waves[slice_index], windows[:, slice_index], propagator)
        window_grad = jnp.stack(object_grads, axis=1)
        current = lax.dynamic_slice(gradient_sum, corner, (2, slices, window_size, window_size))
        return (lax.dynamic_update_slice(gradient_sum, current + window_grad, corner), None)
    initial = jnp.zeros((2, slices, height + window_size, width), jnp.float32)
    gradient_sum, unused = lax.scan(one_position, initial, (positions, intensities))
    folded = gradient_sum[:, :, :height]
    return folded.at[:, :, :window_size].add(gradient_sum[:, :, height:])
```

```python
import functools
import math

import jax
import jax.numpy as jnp
import numpy as np
from jax import lax
from jax.experimental import pallas as pl
from jax.experimental.pallas import tpu as pltpu
from jax.sharding import PartitionSpec as P

MESH = pl.DeviceIdType.MESH
BF16 = jnp.bfloat16
F32 = jnp.float32
REACH = 5
LANES = 128


def dft_table(length):
    serial = np.arange(length, dtype=np.int32)
    angle_index = serial[:, None] * serial[None, :] % length
    angle = angle_index.astype(np.float32) * np.float32(2.0 * math.pi / length)
    scale = np.float32(1.0 / math.sqrt(length))
    return jnp.asarray(
        np.stack([np.cos(angle) * scale, -np.sin(angle) * scale]), dtype=BF16
    )


def place():
    me = lax.axis_index("scan")
    cut = lax.axis_index("cuts")
    return me, cut, lax.rem(me, 2)


def wrapped(index, count):
    return lax.rem(index + 2 * count, count)


def worker(me, d, m, count):
    band = wrapped(me - d, count)
    return wrapped(me - d + 2, count), 2 * lax.rem(band, 2) + m


def column_split(column, width, window):
    base = jnp.minimum(column // LANES * LANES, width - window - LANES)
    return pl.multiple_of(base, LANES), column - base


def positions_kernel(count, pos_ref, pos_out, tile, pos_in, psend, precv):
    me, cut, parity = place()
    barrier = pltpu.get_barrier_semaphore()
    for d in range(1, REACH):
        pl.semaphore_signal(barrier, inc=1, device_id=(wrapped(me - d, count), cut), device_id_type=MESH)
    lane = lax.broadcasted_iota(jnp.int32, (8, LANES), 1)
    values = jnp.zeros((8, LANES), jnp.int32)
    for n in range(4):
        values = jnp.where(lane == n, pos_ref[n // 2, n % 2], values)
    tile[...] = values
    pos_out[0] = values
    pl.semaphore_wait(barrier, REACH - 1)
    copies = []
    for d in range(1, REACH):
        copy = pltpu.make_async_remote_copy(
            src_ref=tile, dst_ref=pos_in.at[d - 1], send_sem=psend.at[d - 1], recv_sem=precv.at[d - 1],
            device_id=(wrapped(me + d, count), cut), device_id_type=MESH)
        copy.start()
        copies.append(copy)
    for d in range(1, REACH):
        copies[d - 1].wait()
        pos_out[d] = pos_in[d - 1]


def pack_kernel(pos_ref, band, stage, band2):
    window = stage.shape[3]
    width = band.shape[3]
    band2[:, :128] = band[:, 0]
    band2[:, 128:] = band[:, 0]
    lane5 = lax.broadcasted_iota(jnp.int32, (5, 8, LANES), 2)
    sub4 = lax.broadcasted_iota(jnp.int32, (4, 8, LANES), 1)
    def pack(slot, row, column):
        offset = lax.rem(row, 128)
        tile_row, low_row = offset // 8, lax.rem(offset, 8)
        base, shift = column_split(column, width, window)
        turn = lax.rem(LANES - shift, LANES)
        lift = lax.rem(8 - low_row, 8)
        keep = lane5 + shift < LANES
        keep_row = sub4 + low_row < 8

        for part in range(2):
            def strip(q, carry):
                rows = pl.ds(pl.multiple_of(tile_row * 8 + q * 32, 8), 40)
                block = band2[part, rows, pl.ds(base, window + LANES)]
                turned = [
                    pltpu.roll(block[:, j * LANES:(j + 1) * LANES].reshape(5, 8, LANES), turn, 2)
                    for j in range(window // LANES + 1)
                ]
                for j in range(window // LANES):
                    lifted = pltpu.roll(jnp.where(keep, turned[j], turned[j + 1]), lift, 1)
                    made = jnp.where(keep_row, lifted[:4], lifted[1:]).reshape(32, LANES)
                    stage[slot, part, pl.ds(pl.multiple_of(q * 32, 32), 32), j * LANES:(j + 1) * LANES] = made.astype(BF16)
                return carry
            lax.fori_loop(0, 4, strip, 0)

    for d in range(REACH):
        for m in range(2):
            pack(d * 2 + m, pos_ref[d, 0, 2 * m], pos_ref[d, 0, 2 * m + 1])


def send_kernel(count, stage, int_ref, win_ref, own_int_ref, win_send, win_recv, self_sem, isend, irecv):
    me, cut, parity = place()
    active = (cut // 2) == parity
    barrier = pltpu.get_barrier_semaphore()

    @pl.when(active)
    def _():
        pl.semaphore_signal(barrier, inc=1, device_id=(wrapped(me - 2, count), cut), device_id_type=MESH)
        for d in range(REACH):
            for k in range(4):
                def greet():
                    pl.semaphore_signal(
                        barrier, inc=1, device_id=(wrapped(me - 2 + d, count), jnp.int32(k)), device_id_type=MESH
                    )
                if d == 2:
                    pl.when(cut != k)(greet)
                else:
                    greet()

    pl.semaphore_wait(barrier, 10)

    icopy = pltpu.make_async_remote_copy(
        src_ref=int_ref.at[lax.rem(cut, 2)], dst_ref=own_int_ref, send_sem=isend, recv_sem=irecv,
        device_id=(wrapped(me + 2, count), cut), device_id_type=MESH)

    def window_copy(d, m):
        slot = d * 2 + m
        scan_to, cut_to = worker(me, d, m, count)
        return pltpu.make_async_remote_copy(
            src_ref=stage.at[slot], dst_ref=win_ref.at[cut, :, pl.ds(d * 128, 128), :],
            send_sem=win_send.at[slot], recv_sem=win_recv.at[cut, d],
            device_id=(scan_to, cut_to), device_id_type=MESH)

    def local_copy(slot):
        return pltpu.make_async_copy(stage.at[slot], win_ref.at[cut, :, pl.ds(256, 128), :], self_sem)

    def send(d, m):
        if d == 2:
            mine = cut == 2 * parity + m
            pl.when(jnp.logical_not(mine))(lambda: window_copy(d, m).start())
            pl.when(mine)(lambda: local_copy(d * 2 + m).start())
        else:
            window_copy(d, m).start()

    for d in range(REACH):
        for m in range(2):
            send(d, m)
    @pl.when(active)
    def _():
        icopy.start()
    for d in range(REACH):
        for m in range(2):
            if d == 2:
                mine = cut == 2 * parity + m
                pl.when(jnp.logical_not(mine))(lambda: window_copy(d, m).wait_send())
                pl.when(mine)(lambda: local_copy(d * 2 + m).wait())
            else:
                window_copy(d, m).wait_send()

    @pl.when(active)
    def _():
        for d in range(REACH):
            for k in range(4):
                def arrive():
                    pltpu.make_async_copy(
                        stage.at[0], win_ref.at[k, :, pl.ds(d * 128, 128), :], win_recv.at[k, d]).wait()
                if d == 2:
                    pl.when(cut != k)(arrive)
                else:
                    arrive()
        icopy.wait()


def chain_kernel(pos_ref, win, probe, prop, table, intensity, out,
                 big_m, big_mt, big_f, big_ft, upright, flat, waves, far):
    me, cut, parity = place()
    size = probe.shape[1]
    slices = win.shape[0]
    active = (cut // 2) == parity

    def dot(a, b):
        return jnp.dot(a, b, preferred_element_type=F32)

    def left(big):
        def step(n, carry):
            cols = pl.ds(pl.multiple_of(n * 256, 256), 256)
            cols_im = pl.ds(pl.multiple_of(size + n * 256, 256), 256)
            got = dot(big[...], upright[:, cols])
            flat[:, cols] = got[:size].astype(BF16)
            flat[:, cols_im] = got[size:].astype(BF16)
            return carry
        lax.fori_loop(0, size // 256, step, 0)

    def right(big, put):
        def step(n, carry):
            cols = pl.ds(pl.multiple_of(n * 256, 256), 256)
            cols_im = pl.ds(pl.multiple_of(size + n * 256, 256), 256)
            put(cols, dot(flat[...], big[:, cols]), dot(flat[...], big[:, cols_im]))
            return carry
        lax.fori_loop(0, size // 256, step, 0)

    @pl.when(active)
    def _():
        offset = lax.rem(pos_ref[2, 0, 2 * lax.rem(cut, 2)], 128)
        for big, big_t, src in ((big_m, big_mt, prop), (big_f, big_ft, table)):
            re, im = src[0], src[1]
            re_t, im_t = re.T, im.T
            big[:size, :size] = re
            big[:size, size:] = -im
            big[size:, :size] = im
            big[size:, size:] = re
            big_t[:size, :size] = re_t
            big_t[:size, size:] = im_t
            big_t[size:, :size] = -im_t
            big_t[size:, size:] = re_t
        waves[0] = probe[...]

        def window_rows(s, part, e, cols, width):
            row = lax.broadcasted_iota(jnp.int32, (128, width), 0)
            top = win[s, part, pl.ds(pl.multiple_of(e * 128, 128), 128), cols].astype(F32)
            low = win[s, part, pl.ds(pl.multiple_of(e * 128 + 128, 128), 128), cols].astype(F32)
            return jnp.where(row < 128 - offset, top, low)

        def mix(s):
            def strip(n, carry):
                e = n // 4
                cols = pl.ds(pl.multiple_of(lax.rem(n, 4) * 128, 128), 128)
                rows = pl.ds(pl.multiple_of(e * 128, 128), 128)
                rows_im = pl.ds(pl.multiple_of(size + e * 128, 128), 128)
                w_re, w_im = window_rows(s, 0, e, cols, 128), window_rows(s, 1, e, cols, 128)
                p_re, p_im = waves[s, 0, rows, cols].astype(F32), waves[s, 1, rows, cols].astype(F32)
                upright[rows, cols] = (p_re * w_re - p_im * w_im).astype(BF16)
                upright[rows_im, cols] = (p_re * w_im + p_im * w_re).astype(BF16)
                return carry
            lax.fori_loop(0, 16, strip, 0)

        def forward(s, carry):
            mix(s)
            left(big_m)

            def put(cols, re, im):
                waves[s + 1, 0, :, cols] = re.astype(BF16)
                waves[s + 1, 1, :, cols] = im.astype(BF16)
            right(big_mt, put)
            return carry
        lax.fori_loop(0, slices, forward, 0)

        upright[:size] = waves[slices, 0]
        upright[size:] = waves[slices, 1]
        left(big_f)

        def put_far(cols, re, im):
            excess = re * re + im * im - intensity[:, cols]
            upright[:size, cols] = (excess * re).astype(BF16)
            upright[size:, cols] = (excess * im).astype(BF16)
        right(big_ft, put_far)
        left(big_ft)

        def put_last(cols, re, im):
            far[0, :, cols] = re.astype(BF16)
            far[1, :, cols] = im.astype(BF16)
        right(big_f, put_last)
        flat[:, :size] = far[0]
        flat[:, size:] = far[1]

        def backward(n, carry):
            s = slices - 1 - n

            def put_half(cols, re, im):
                upright[:size, cols] = re.astype(BF16)
                upright[size:, cols] = im.astype(BF16)
            right(big_m, put_half)

            def tile(n, carry):
                cols = pl.ds(pl.multiple_of(n * 256, 256), 256)
                cols_im = pl.ds(pl.multiple_of(size + n * 256, 256), 256)
                got = dot(big_mt[...], upright[:, cols])
                row = lax.broadcasted_iota(jnp.int32, (128, 256), 0)
                head = row < 128 - offset
                last_re = jnp.zeros((128, 256), F32)
                last_im = jnp.zeros((128, 256), F32)
                for e in range(4):
                    g_re = got[e * 128:(e + 1) * 128]
                    g_im = got[size + e * 128:size + (e + 1) * 128]
                    rows = slice(e * 128, (e + 1) * 128)
                    p_re, p_im = waves[s, 0, rows, cols].astype(F32), waves[s, 1, rows, cols].astype(F32)
                    w_re, w_im = window_rows(s, 0, e, cols, 256), window_rows(s, 1, e, cols, 256)
                    o_re = p_re * g_re + p_im * g_im
                    o_im = p_re * g_im - p_im * g_re
                    out[s, e, 0, :, cols] = jnp.where(head, o_re, last_re).astype(BF16)
                    out[s, e, 1, :, cols] = jnp.where(head, o_im, last_im).astype(BF16)
                    last_re, last_im = o_re, o_im
                    flat[rows, cols] = (w_re * g_re + w_im * g_im).astype(BF16)
                    flat[rows, cols_im] = (w_re * g_im - w_im * g_re).astype(BF16)
                out[s, 4, 0, :, cols] = jnp.where(head, 0.0, last_re).astype(BF16)
                out[s, 4, 1, :, cols] = jnp.where(head, 0.0, last_im).astype(BF16)
                return carry
            lax.fori_loop(0, size // 256, tile, 0)
            return carry
        lax.fori_loop(0, slices, backward, 0)


def return_kernel(count, blocks, got, send_sems, recv_sems, self_sem):
    me, cut, parity = place()
    active = (cut // 2) == parity
    barrier = pltpu.get_barrier_semaphore()
    for d in range(REACH):
        for m in range(2):
            def greet():
                pl.semaphore_signal(barrier, inc=1, device_id=worker(me, d, m, count), device_id_type=MESH)
            if d == 2:
                pl.when(cut != 2 * parity + m)(greet)
            else:
                greet()

    def copy_of(d, k):
        return pltpu.make_async_remote_copy(
            src_ref=blocks.at[k, d], dst_ref=got.at[d, lax.rem(cut, 2)],
            send_sem=send_sems.at[k, d], recv_sem=recv_sems.at[d, lax.rem(cut, 2)],
            device_id=(wrapped(me - 2 + d, count), jnp.int32(k)), device_id_type=MESH)

    def local_copy(k):
        return pltpu.make_async_copy(blocks.at[k, 2], got.at[2, lax.rem(cut, 2)], self_sem)

    @pl.when(active)
    def _():
        pl.semaphore_wait(barrier, 19)
        for d in (0, 4, 1, 3, 2):
            for k in range(4):
                if d == 2:
                    pl.when(cut != k)(lambda: copy_of(d, k).start())
                    pl.when(cut == k)(lambda: local_copy(k).start())
                else:
                    copy_of(d, k).start()
        for d in range(REACH):
            for k in range(4):
                if d == 2:
                    pl.when(cut != k)(lambda: copy_of(d, k).wait_send())
                    pl.when(cut == k)(lambda: local_copy(k).wait())
                else:
                    copy_of(d, k).wait_send()

    for d in range(REACH):
        for m in range(2):
            def arrive():
                pltpu.make_async_copy(blocks.at[0, 0], got.at[d, m], recv_sems.at[d, m]).wait()
            if d == 2:
                pl.when(cut != 2 * parity + m)(arrive)
            else:
                arrive()


def add_kernel(pos_ref, got, out, acc):
    width = out.shape[3]
    window = got.shape[4]
    acc[...] = jnp.zeros_like(acc)
    lane = lax.broadcasted_iota(jnp.int32, (4, 8, LANES), 2)
    sub = lax.broadcasted_iota(jnp.int32, (5, 8, LANES), 1)
    count = window // LANES
    zero = jnp.zeros((4, 8, LANES), F32)
    gap = jnp.zeros((1, 8, LANES), F32)
    for d in range(REACH):
        for m in range(2):
            offset = lax.rem(pos_ref[d, 0, 2 * m], 128)
            tile_row, low_row = offset // 8, lax.rem(offset, 8)
            base, shift = column_split(pos_ref[d, 0, 2 * m + 1], width, window)
            turn = lax.rem(shift, LANES)
            keep = lane >= shift
            keep_row = sub >= low_row
            for part in range(2):
                def strip(q, carry):
                    rows = pl.ds(pl.multiple_of(q * 32, 32), 32)
                    turned = [
                        pltpu.roll(
                            got[d, m, part, rows, j * LANES:(j + 1) * LANES].astype(F32).reshape(4, 8, LANES), turn, 2)
                        for j in range(count)
                    ]
                    made = []
                    for j in range(count + 1):
                        here = turned[j] if j < count else zero
                        before = turned[j - 1] if j > 0 else zero
                        moved = pltpu.roll(jnp.where(keep, here, before), low_row, 1)
                        made.append(jnp.where(
                            keep_row, jnp.concatenate([moved, gap]), jnp.concatenate([gap, moved])).reshape(40, LANES))
                    to_rows = pl.ds(pl.multiple_of(tile_row * 8 + q * 32, 8), 40)
                    for j in range(count + 1):
                        to_cols = pl.ds(pl.multiple_of(base + j * LANES, LANES), LANES)
                        acc[part, to_rows, to_cols] += made[j]
                    return carry
                lax.fori_loop(0, 4, strip, 0)
    out[:, 0] = acc[:, :128] + acc[:, 128:]


def local(probe_wave, propagator, object_slices, positions, intensities):
    count = lax.axis_size("scan")
    size = probe_wave.shape[1]
    vmem = pl.BlockSpec(memory_space=pltpu.VMEM)
    smem = pl.BlockSpec(memory_space=pltpu.SMEM)
    anywhere = pl.BlockSpec(memory_space=pl.ANY)
    dma = pltpu.SemaphoreType.DMA
    pos = pl.pallas_call(
        functools.partial(positions_kernel, count),
        out_shape=jax.ShapeDtypeStruct((REACH, 8, LANES), jnp.int32),
        in_specs=[smem],
        out_specs=vmem,
        scratch_shapes=[
            pltpu.VMEM((8, LANES), jnp.int32), pltpu.VMEM((4, 8, LANES), jnp.int32), dma((4,)), dma((4,))],
        compiler_params=pltpu.CompilerParams(
            collective_id=0, has_side_effects=True, vmem_limit_bytes=4 * 2**20),
        name="share_positions",
    )(positions)

    stage = pl.pallas_call(
        pack_kernel,
        out_shape=jax.ShapeDtypeStruct((10, 2, 128, size), BF16),
        in_specs=[smem, vmem],
        out_specs=vmem,
        scratch_shapes=[pltpu.VMEM((2, 256, object_slices.shape[3]), F32)],
        compiler_params=pltpu.CompilerParams(vmem_limit_bytes=24 * 2**20),
        name="pack_windows",
    )(pos, object_slices)

    windows, own_int = pl.pallas_call(
        functools.partial(send_kernel, count),
        out_shape=[
            jax.ShapeDtypeStruct((4, 2, REACH * 128, size), BF16),
            jax.ShapeDtypeStruct((size, size), F32),
        ],
        in_specs=[anywhere, anywhere],
        out_specs=[anywhere, anywhere],
        scratch_shapes=[dma((10,)), dma((4, REACH)), dma, dma, dma],
        compiler_params=pltpu.CompilerParams(
            collective_id=1, has_side_effects=True, vmem_limit_bytes=24 * 2**20),
        name="send_windows",
    )(stage, intensities)

    blocks = pl.pallas_call(
        chain_kernel,
        out_shape=jax.ShapeDtypeStruct((4, REACH, 2, 128, size), BF16),
        in_specs=[smem] + [vmem] * 5,
        out_specs=vmem,
        scratch_shapes=[pltpu.VMEM((2 * size, 2 * size), BF16)] * 4
        + [
            pltpu.VMEM((2 * size, size), BF16),
            pltpu.VMEM((size, 2 * size), BF16),
            pltpu.VMEM((5, 2, size, size), BF16),
            pltpu.VMEM((2, size, size), BF16),
        ],
        compiler_params=pltpu.CompilerParams(vmem_limit_bytes=56 * 2**20),
        name="chain",
    )(pos, windows, probe_wave, propagator, dft_table(size), own_int)

    got = pl.pallas_call(
        functools.partial(return_kernel, count),
        out_shape=jax.ShapeDtypeStruct((REACH, 2, 2, 128, size), BF16),
        in_specs=[anywhere],
        out_specs=anywhere,
        scratch_shapes=[dma((4, REACH)), dma((REACH, 2)), dma],
        compiler_params=pltpu.CompilerParams(
            collective_id=2, has_side_effects=True, vmem_limit_bytes=24 * 2**20),
        name="return_gradients",
    )(blocks)

    return pl.pallas_call(
        add_kernel,
        out_shape=jax.ShapeDtypeStruct(object_slices.shape, F32),
        in_specs=[smem, vmem],
        out_specs=vmem,
        scratch_shapes=[pltpu.VMEM((2, 256, object_slices.shape[3]), F32)],
        compiler_params=pltpu.CompilerParams(vmem_limit_bytes=24 * 2**20),
        name="add_gradients",
    )(pos, got)


def solution(mesh):
    in_specs = (P(), P(), P(None, "cuts", "scan", None), P("scan", None), P("scan", None, None))
    out_specs = P(None, "cuts", "scan", None)
    return jax.shard_map(local, mesh=mesh, in_specs=in_specs, out_specs=out_specs, check_vma=False)
```

```python
import functools
import math

import jax
import jax.numpy as jnp
import numpy as np
from jax import lax
from jax.experimental import pallas as pl
from jax.experimental.pallas import tpu as pltpu
from jax.sharding import PartitionSpec as P

MESH = pl.DeviceIdType.MESH
BF16 = jnp.bfloat16
F32 = jnp.float32
REACH = 5
LANES = 128
ORDER = (0, 4, 1, 3, 2)


def dft_table(length):
    serial = np.arange(length, dtype=np.int32)
    angle_index = serial[:, None] * serial[None, :] % length
    angle = angle_index.astype(np.float32) * np.float32(2.0 * math.pi / length)
    scale = np.float32(1.0 / math.sqrt(length))
    return jnp.asarray(
        np.stack([np.cos(angle) * scale, -np.sin(angle) * scale]), dtype=BF16
    )


def place():
    me = lax.axis_index("scan")
    cut = lax.axis_index("cuts")
    return me, cut, lax.rem(me, 2)


def wrapped(index, count):
    return lax.rem(index + 2 * count, count)


def worker(me, d, m, count):
    band = wrapped(me - d, count)
    return wrapped(me - d + 2, count), 2 * lax.rem(band, 2) + m


def column_split(column, width, window):
    base = jnp.minimum(column // LANES * LANES, width - window - LANES)
    return pl.multiple_of(base, LANES), column - base


def positions_kernel(count, pos_ref, pos_out, tile, pos_in, psend, precv):
    me, cut, parity = place()
    barrier = pltpu.get_barrier_semaphore()
    for d in range(1, REACH):
        pl.semaphore_signal(barrier, inc=1, device_id=(wrapped(me - d, count), cut), device_id_type=MESH)
    lane = lax.broadcasted_iota(jnp.int32, (8, LANES), 1)
    values = jnp.zeros((8, LANES), jnp.int32)
    for n in range(4):
        values = jnp.where(lane == n, pos_ref[n // 2, n % 2], values)
    tile[...] = values
    pos_out[0] = values
    pl.semaphore_wait(barrier, REACH - 1)
    copies = []
    for d in range(1, REACH):
        copy = pltpu.make_async_remote_copy(
            src_ref=tile, dst_ref=pos_in.at[d - 1], send_sem=psend.at[d - 1], recv_sem=precv.at[d - 1],
            device_id=(wrapped(me + d, count), cut), device_id_type=MESH)
        copy.start()
        copies.append(copy)
    for d in range(1, REACH):
        copies[d - 1].wait()
        pos_out[d] = pos_in[d - 1]


def pack_kernel(pos_ref, band, stage, band2):
    window = stage.shape[3]
    width = band.shape[3]
    band2[:, :128] = band[:, 0]
    band2[:, 128:] = band[:, 0]
    lane = lax.broadcasted_iota(jnp.int32, (17, 8, LANES), 2)
    sub = lax.broadcasted_iota(jnp.int32, (16, 8, LANES), 1)
    for d in range(REACH):
        for m in range(2):
            offset = lax.rem(pos_ref[d, 0, 2 * m], 128)
            tile_row, low_row = offset // 8, lax.rem(offset, 8)
            base, shift = column_split(pos_ref[d, 0, 2 * m + 1], width, window)
            turn = lax.rem(LANES - shift, LANES)
            lift = lax.rem(8 - low_row, 8)
            keep = lane + shift < LANES
            keep_row = sub + low_row < 8
            rows = pl.ds(pl.multiple_of(tile_row * 8, 8), 136)
            for part in range(2):
                turned = []
                for j in range(window // LANES + 1):
                    cols = pl.ds(pl.multiple_of(base + j * LANES, LANES), LANES)
                    turned.append(pltpu.roll(band2[part, rows, cols].reshape(17, 8, LANES), turn, 2))
                for j in range(window // LANES):
                    lifted = pltpu.roll(jnp.where(keep, turned[j], turned[j + 1]), lift, 1)
                    made = jnp.where(keep_row, lifted[:16], lifted[1:]).reshape(128, LANES)
                    stage[d * 2 + m, part, :, j * LANES:(j + 1) * LANES] = made.astype(BF16)


def chain_kernel(count, row_ref, stage, int_ref, probe, prop, table, got,
                 win, intensity, out, big_m, big_mt, big_f, big_ft, upright, flat, waves,
                 win_send, win_recv, self_sem, isend, irecv, out_send, out_recv, out_self):
    me, cut, parity = place()
    size = probe.shape[1]
    slices = win.shape[0]
    active = (cut // 2) == parity
    half = lax.rem(cut, 2)

    def owner(d, k):
        return wrapped(me - 2 + d, count), jnp.int32(k)

    def is_self(d, m):
        return cut == 2 * parity + m if d == 2 else None

    def either(same, remote, here):
        if same is None:
            remote()
        else:
            pl.when(jnp.logical_not(same))(remote)
            if here is not None:
                pl.when(same)(here)

    barrier = pltpu.get_barrier_semaphore()

    def greet(device):
        pl.semaphore_signal(barrier, inc=1, device_id=device, device_id_type=MESH)

    for d in range(REACH):
        for m in range(2):
            either(is_self(d, m), lambda: greet(worker(me, d, m, count)), None)

    @pl.when(active)
    def _():
        greet((wrapped(me - 2, count), cut))
        for d in range(REACH):
            for k in range(4):
                either(cut == k if d == 2 else None, lambda: greet(owner(d, k)), None)

    pl.semaphore_wait(barrier, jnp.where(active, 29, 10))

    def window_copy(d, m):
        return pltpu.make_async_remote_copy(
            src_ref=stage.at[d * 2 + m], dst_ref=win.at[cut, :, pl.ds(d * 128, 128), :],
            send_sem=win_send.at[d * 2 + m], recv_sem=win_recv.at[cut, d],
            device_id=worker(me, d, m, count), device_id_type=MESH)

    def window_here(m):
        return pltpu.make_async_copy(stage.at[4 + m], win.at[cut, :, pl.ds(256, 128), :], self_sem)

    def window_arrival(s, d):
        return pltpu.make_async_copy(stage.at[0], win.at[s, :, pl.ds(d * 128, 128), :], win_recv.at[s, d])

    def block_copy(d, k):
        return pltpu.make_async_remote_copy(
            src_ref=out.at[k, d], dst_ref=got.at[d, half],
            send_sem=out_send.at[k, d], recv_sem=out_recv.at[d, half],
            device_id=owner(d, k), device_id_type=MESH)

    def block_here():
        return pltpu.make_async_copy(out.at[cut, 2], got.at[2, half], out_self)

    icopy = pltpu.make_async_remote_copy(
        src_ref=int_ref.at[half], dst_ref=intensity, send_sem=isend, recv_sem=irecv,
        device_id=(wrapped(me + 2, count), cut), device_id_type=MESH)

    for d in ORDER:
        for m in range(2):
            either(is_self(d, m), lambda: window_copy(d, m).start(), lambda: window_here(m).start())

    def dot(a, b):
        return jnp.dot(a, b, preferred_element_type=F32)

    def left(big):
        made = dot(big[...], upright[...])
        flat[:, :size] = made[:size].astype(BF16)
        flat[:, size:] = made[size:].astype(BF16)

    @pl.when(active)
    def _():
        icopy.start()
        offset = lax.rem(row_ref[2, 0, 2 * half], 128)
        for big, big_t, src in ((big_m, big_mt, prop), (big_f, big_ft, table)):
            re, im = src[0], src[1]
            re_t, im_t = re.T, im.T
            big[:size, :size] = re
            big[:size, size:] = -im
            big[size:, :size] = im
            big[size:, size:] = re
            big_t[:size, :size] = re_t
            big_t[:size, size:] = im_t
            big_t[size:, :size] = -im_t
            big_t[size:, size:] = re_t
        waves[0] = probe[...]
        head = lax.broadcasted_iota(jnp.int32, (128, size), 0) < 128 - offset

        def window_rows(s, part, e):
            top = win[s, part, e * 128:(e + 1) * 128, :].astype(F32)
            low = win[s, part, (e + 1) * 128:(e + 2) * 128, :].astype(F32)
            return jnp.where(head, top, low)

        def forward(s, carry):
            for d in range(REACH):
                either(cut == s if d == 2 else None,
                       lambda: window_arrival(s, d).wait(), lambda: window_here(half).wait())
            for e in range(4):
                rows = slice(e * 128, (e + 1) * 128)
                rows_im = slice(size + e * 128, size + (e + 1) * 128)
                w_re, w_im = window_rows(s, 0, e), window_rows(s, 1, e)
                p_re, p_im = waves[s, 0, rows].astype(F32), waves[s, 1, rows].astype(F32)
                upright[rows] = (p_re * w_re - p_im * w_im).astype(BF16)
                upright[rows_im] = (p_re * w_im + p_im * w_re).astype(BF16)
            left(big_m)
            made = dot(flat[...], big_mt[...])
            waves[s + 1, 0] = made[:, :size].astype(BF16)
            waves[s + 1, 1] = made[:, size:].astype(BF16)
            return carry
        lax.fori_loop(0, slices, forward, 0)

        upright[:size] = waves[slices, 0]
        upright[size:] = waves[slices, 1]
        left(big_f)
        icopy.wait()
        made = dot(flat[...], big_ft[...])
        for e in range(4):
            rows = slice(e * 128, (e + 1) * 128)
            re, im = made[rows, :size], made[rows, size:]
            excess = re * re + im * im - intensity[rows]
            upright[rows] = (excess * re).astype(BF16)
            upright[size + e * 128:size + (e + 1) * 128] = (excess * im).astype(BF16)
        left(big_ft)
        flat[...] = dot(flat[...], big_f[...]).astype(BF16)

        def backward(n, carry):
            s = slices - 1 - n
            made = dot(flat[...], big_m[...])
            upright[:size] = made[:, :size].astype(BF16)
            upright[size:] = made[:, size:].astype(BF16)
            made = dot(big_mt[...], upright[...])
            last_re = jnp.zeros((128, size), F32)
            last_im = jnp.zeros((128, size), F32)
            for e in range(4):
                rows = slice(e * 128, (e + 1) * 128)
                g_re, g_im = made[rows], made[size + e * 128:size + (e + 1) * 128]
                p_re, p_im = waves[s, 0, rows].astype(F32), waves[s, 1, rows].astype(F32)
                o_re = p_re * g_re + p_im * g_im
                o_im = p_re * g_im - p_im * g_re
                out[s, e, 0] = jnp.where(head, o_re, last_re).astype(BF16)
                out[s, e, 1] = jnp.where(head, o_im, last_im).astype(BF16)
                last_re, last_im = o_re, o_im
                w_re, w_im = window_rows(s, 0, e), window_rows(s, 1, e)
                flat[rows, :size] = (w_re * g_re + w_im * g_im).astype(BF16)
                flat[rows, size:] = (w_re * g_im - w_im * g_re).astype(BF16)
            out[s, 4, 0] = jnp.where(head, 0.0, last_re).astype(BF16)
            out[s, 4, 1] = jnp.where(head, 0.0, last_im).astype(BF16)
            for d in ORDER:
                either(cut == s if d == 2 else None,
                       lambda: block_copy(d, s).start(), lambda: block_here().start())
            return carry
        lax.fori_loop(0, slices, backward, 0)

    for d in range(REACH):
        for m in range(2):
            either(is_self(d, m), lambda: window_copy(d, m).wait_send(), None)

    @pl.when(active)
    def _():
        for d in range(REACH):
            for k in range(4):
                either(cut == k if d == 2 else None,
                       lambda: block_copy(d, k).wait_send(), lambda: block_here().wait())

    for d in range(REACH):
        for m in range(2):
            either(is_self(d, m),
                   lambda: pltpu.make_async_copy(out.at[0, 0], got.at[d, m], out_recv.at[d, m]).wait(), None)


def add_kernel(pos_ref, got, out, acc):
    width = out.shape[3]
    window = got.shape[4]
    acc[...] = jnp.zeros_like(acc)
    lane = lax.broadcasted_iota(jnp.int32, (16, 8, LANES), 2)
    sub = lax.broadcasted_iota(jnp.int32, (17, 8, LANES), 1)
    count = window // LANES
    zero = jnp.zeros((16, 8, LANES), F32)
    gap = jnp.zeros((1, 8, LANES), F32)
    for d in range(REACH):
        for m in range(2):
            offset = lax.rem(pos_ref[d, 0, 2 * m], 128)
            tile_row, low_row = offset // 8, lax.rem(offset, 8)
            base, shift = column_split(pos_ref[d, 0, 2 * m + 1], width, window)
            turn = lax.rem(shift, LANES)
            keep = lane >= shift
            keep_row = sub >= low_row
            to_rows = pl.ds(pl.multiple_of(tile_row * 8, 8), 136)
            for part in range(2):
                before = zero
                for j in range(count + 1):
                    here = zero
                    if j < count:
                        here = pltpu.roll(
                            got[d, m, part, :, j * LANES:(j + 1) * LANES].astype(F32).reshape(16, 8, LANES), turn, 2)
                    moved = pltpu.roll(jnp.where(keep, here, before), low_row, 1)
                    before = here
                    made = jnp.where(keep_row, jnp.concatenate([moved, gap]), jnp.concatenate([gap, moved]))
                    to_cols = pl.ds(pl.multiple_of(base + j * LANES, LANES), LANES)
                    acc[part, to_rows, to_cols] += made.reshape(136, LANES)
    out[:, 0] = acc[:, :128] + acc[:, 128:]


def local(probe_wave, propagator, object_slices, positions, intensities):
    count = lax.axis_size("scan")
    size = probe_wave.shape[1]
    vmem = pl.BlockSpec(memory_space=pltpu.VMEM)
    smem = pl.BlockSpec(memory_space=pltpu.SMEM)
    anywhere = pl.BlockSpec(memory_space=pl.ANY)
    dma = pltpu.SemaphoreType.DMA
    pos = pl.pallas_call(
        functools.partial(positions_kernel, count),
        out_shape=jax.ShapeDtypeStruct((REACH, 8, LANES), jnp.int32),
        in_specs=[smem],
        out_specs=vmem,
        scratch_shapes=[
            pltpu.VMEM((8, LANES), jnp.int32), pltpu.VMEM((4, 8, LANES), jnp.int32), dma((4,)), dma((4,))],
        compiler_params=pltpu.CompilerParams(
            collective_id=0, has_side_effects=True, vmem_limit_bytes=4 * 2**20),
        name="share_positions",
    )(positions)

    stage = pl.pallas_call(
        pack_kernel,
        out_shape=jax.ShapeDtypeStruct((10, 2, 128, size), BF16),
        in_specs=[smem, vmem],
        out_specs=vmem,
        scratch_shapes=[pltpu.VMEM((2, 256, object_slices.shape[3]), F32)],
        compiler_params=pltpu.CompilerParams(vmem_limit_bytes=24 * 2**20),
        name="pack_windows",
    )(pos, object_slices)

    got = pl.pallas_call(
        functools.partial(chain_kernel, count),
        out_shape=jax.ShapeDtypeStruct((REACH, 2, 2, 128, size), BF16),
        in_specs=[smem, vmem, anywhere, vmem, vmem, vmem],
        out_specs=anywhere,
        scratch_shapes=[
            pltpu.VMEM((4, 2, REACH * 128, size), BF16),
            pltpu.VMEM((size, size), F32),
            pltpu.VMEM((4, REACH, 2, 128, size), BF16),
        ]
        + [pltpu.VMEM((2 * size, 2 * size), BF16)] * 4
        + [
            pltpu.VMEM((2 * size, size), BF16),
            pltpu.VMEM((size, 2 * size), BF16),
            pltpu.VMEM((5, 2, size, size), BF16),
            dma((10,)), dma((4, REACH)), dma, dma, dma, dma((4, REACH)), dma((REACH, 2)), dma,
        ],
        compiler_params=pltpu.CompilerParams(
            collective_id=1, has_side_effects=True, vmem_limit_bytes=52 * 2**20),
        name="chain",
    )(pos, stage, intensities, probe_wave, propagator, dft_table(size))

    return pl.pallas_call(
        add_kernel,
        out_shape=jax.ShapeDtypeStruct(object_slices.shape, F32),
        in_specs=[smem, vmem],
        out_specs=vmem,
        scratch_shapes=[pltpu.VMEM((2, 256, object_slices.shape[3]), F32)],
        compiler_params=pltpu.CompilerParams(vmem_limit_bytes=24 * 2**20),
        name="add_gradients",
    )(pos, got)


def solution(mesh):
    in_specs = (P(), P(), P(None, "cuts", "scan", None), P("scan", None), P("scan", None, None))
    out_specs = P(None, "cuts", "scan", None)
    return jax.shard_map(local, mesh=mesh, in_specs=in_specs, out_specs=out_specs, check_vma=False)
```

```python
import functools
import math

import jax
import jax.numpy as jnp
import numpy as np
from jax import lax
from jax.experimental import pallas as pl
from jax.experimental.pallas import tpu as pltpu
from jax.sharding import PartitionSpec as P

MESH = pl.DeviceIdType.MESH
BF16 = jnp.bfloat16
F32 = jnp.float32
REACH = 5
LANES = 128


def dft_table(length):
    serial = np.arange(length, dtype=np.int32)
    angle_index = serial[:, None] * serial[None, :] % length
    angle = angle_index.astype(np.float32) * np.float32(2.0 * math.pi / length)
    scale = np.float32(1.0 / math.sqrt(length))
    return jnp.asarray(
        np.stack([np.cos(angle) * scale, -np.sin(angle) * scale]), dtype=BF16
    )


def place():
    me = lax.axis_index("scan")
    cut = lax.axis_index("cuts")
    return me, cut, lax.rem(me, 2)


def wrapped(index, count):
    return lax.rem(index + 2 * count, count)


def worker(me, d, m, count):
    band = wrapped(me - d, count)
    return wrapped(me - d + 2, count), 2 * lax.rem(band, 2) + m


def column_split(column, width, window):
    base = jnp.minimum(column // LANES * LANES, width - window - LANES)
    return pl.multiple_of(base, LANES), column - base


def positions_kernel(count, pos_ref, pos_out, tile, pos_in, psend, precv):
    me, cut, parity = place()
    barrier = pltpu.get_barrier_semaphore()
    for d in range(1, REACH):
        pl.semaphore_signal(barrier, inc=1, device_id=(wrapped(me - d, count), cut), device_id_type=MESH)
    lane = lax.broadcasted_iota(jnp.int32, (8, LANES), 1)
    values = jnp.zeros((8, LANES), jnp.int32)
    for n in range(4):
        values = jnp.where(lane == n, pos_ref[n // 2, n % 2], values)
    tile[...] = values
    pos_out[0] = values
    pl.semaphore_wait(barrier, REACH - 1)
    copies = []
    for d in range(1, REACH):
        copy = pltpu.make_async_remote_copy(
            src_ref=tile, dst_ref=pos_in.at[d - 1], send_sem=psend.at[d - 1], recv_sem=precv.at[d - 1],
            device_id=(wrapped(me + d, count), cut), device_id_type=MESH)
        copy.start()
        copies.append(copy)
    for d in range(1, REACH):
        copies[d - 1].wait()
        pos_out[d] = pos_in[d - 1]


def pack_kernel(pos_ref, band, stage, band2, load_sem):
    window = stage.shape[3]
    width = band.shape[3]
    loads = [
        pltpu.make_async_copy(band.at[:, 0], band2.at[:, pl.ds(h * 128, 128), :], load_sem.at[h])
        for h in range(2)
    ]
    for load in loads:
        load.start()
    for load in loads:
        load.wait()
    lane = lax.broadcasted_iota(jnp.int32, (17, 8, LANES), 2)
    sub = lax.broadcasted_iota(jnp.int32, (16, 8, LANES), 1)
    for d in range(REACH):
        for m in range(2):
            offset = lax.rem(pos_ref[d, 0, 2 * m], 128)
            tile_row, low_row = offset // 8, lax.rem(offset, 8)
            base, shift = column_split(pos_ref[d, 0, 2 * m + 1], width, window)
            turn = lax.rem(LANES - shift, LANES)
            lift = lax.rem(8 - low_row, 8)
            keep = lane + shift < LANES
            keep_row = sub + low_row < 8
            rows = pl.ds(pl.multiple_of(tile_row * 8, 8), 136)
            for part in range(2):
                turned = []
                for j in range(window // LANES + 1):
                    cols = pl.ds(pl.multiple_of(base + j * LANES, LANES), LANES)
                    turned.append(pltpu.roll(band2[part, rows, cols].reshape(17, 8, LANES), turn, 2))
                for j in range(window // LANES):
                    lifted = pltpu.roll(jnp.where(keep, turned[j], turned[j + 1]), lift, 1)
                    made = jnp.where(keep_row, lifted[:16], lifted[1:]).reshape(128, LANES)
                    stage[d * 2 + m, part, :, j * LANES:(j + 1) * LANES] = made.astype(BF16)


def chain_kernel(count, row_ref, stage, int_ref, probe_ref, prop_ref, table_ref, got,
                 win, intensity, out, edge, cross, back, prop, table,
                 big_m, big_mt, big_f, big_ft, upright, flat, waves,
                 load_sem, win_send, win_recv, self_sem, edge_send, edge_recv, cross_send, cross_self,
                 isend, irecv, out_send, out_recv, out_self, back_send, back_recv, back_self, last_send):
    me, cut, parity = place()
    size = flat.shape[0]
    slices = win.shape[0]
    active = (cut // 2) == parity
    half = lax.rem(cut, 2)
    behind, ahead = wrapped(me - 2, count), wrapped(me + 2, count)

    def owner(d, k):
        return wrapped(me - 2 + d, count), jnp.int32(k)

    def is_self(d, m):
        return cut == 2 * parity + m if d == 2 else None

    def either(same, remote, here):
        if same is None:
            remote()
        else:
            pl.when(jnp.logical_not(same))(remote)
            if here is not None:
                pl.when(same)(here)

    loads = [
        pltpu.make_async_copy(src, dst, load_sem.at[n])
        for n, (src, dst) in enumerate(((probe_ref, waves.at[0]), (prop_ref, prop), (table_ref, table)))
    ]
    for load in loads:
        load.start()

    barrier = pltpu.get_barrier_semaphore()

    def greet(device):
        pl.semaphore_signal(barrier, inc=1, device_id=device, device_id_type=MESH)

    greet((behind, cut))
    greet((ahead, cut))
    for m in range(2):
        for d in (1, 2, 3):
            either(is_self(d, m), lambda: greet(worker(me, d, m, count)), None)
        either(is_self(2, m), lambda: greet(worker(me, 2, m, count)), None)

    @pl.when(active)
    def _():
        for k in range(4):
            for d in (1, 2, 3):
                either(cut == k if d == 2 else None, lambda: greet(owner(d, k)), None)
            either(cut == k, lambda: greet(owner(2, k)), None)

    pl.semaphore_wait(barrier, jnp.where(active, 22, 10))

    def unit(s, e):
        return win.at[s, :, pl.ds(e * 128, 128), :]

    def window_copy(d, m):
        return pltpu.make_async_remote_copy(
            src_ref=stage.at[d * 2 + m], dst_ref=unit(cut, d),
            send_sem=win_send.at[d * 2 + m], recv_sem=win_recv.at[cut, d],
            device_id=worker(me, d, m, count), device_id_type=MESH)

    def window_here(m):
        return pltpu.make_async_copy(stage.at[4 + m], unit(cut, 2), self_sem)

    def edge_copy(n):
        return pltpu.make_async_remote_copy(
            src_ref=stage.at[pl.ds(8 * n, 2)], dst_ref=edge.at[n],
            send_sem=edge_send.at[n], recv_sem=edge_recv.at[n],
            device_id=((ahead, behind)[n], cut), device_id_type=MESH)

    def cross_copy(m):
        return pltpu.make_async_remote_copy(
            src_ref=cross.at[m], dst_ref=unit(cut, 0), send_sem=cross_send.at[m], recv_sem=win_recv.at[cut, 0],
            device_id=(me, 2 * parity + m), device_id_type=MESH)

    def cross_here(m):
        return pltpu.make_async_copy(cross.at[m], unit(cut, 0), cross_self)

    def window_arrival(s, e):
        return pltpu.make_async_copy(stage.at[0], unit(s, e), win_recv.at[s, e])

    def block_copy(d, k):
        return pltpu.make_async_remote_copy(
            src_ref=out.at[k, d], dst_ref=got.at[d, half],
            send_sem=out_send.at[k, d], recv_sem=out_recv.at[d, half],
            device_id=owner(d, k), device_id_type=MESH)

    def block_here():
        return pltpu.make_async_copy(out.at[cut, 2], got.at[2, half], out_self)

    def back_copy(k):
        return pltpu.make_async_remote_copy(
            src_ref=out.at[k, 0], dst_ref=back.at[half], send_sem=back_send.at[k], recv_sem=back_recv.at[half],
            device_id=(me, jnp.int32(k)), device_id_type=MESH)

    def back_here():
        return pltpu.make_async_copy(out.at[cut, 0], back.at[half], back_self)

    def last_copy(m, n):
        return pltpu.make_async_remote_copy(
            src_ref=back.at[m], dst_ref=got.at[4 * n, m], send_sem=last_send.at[m, n], recv_sem=out_recv.at[4 * n, m],
            device_id=((behind, ahead)[n], cut), device_id_type=MESH)

    icopy = pltpu.make_async_remote_copy(
        src_ref=int_ref.at[half], dst_ref=intensity, send_sem=isend, recv_sem=irecv,
        device_id=(ahead, cut), device_id_type=MESH)

    for n in range(2):
        edge_copy(n).start()
    for d in (1, 3, 2):
        for m in range(2):
            either(is_self(d, m), lambda: window_copy(d, m).start(), lambda: window_here(m).start())

    def dot(a, b):
        return jnp.dot(a, b, preferred_element_type=F32)

    def left(big):
        made = dot(big[...], upright[...])
        flat[:, :size] = made[:size].astype(BF16)
        flat[:, size:] = made[size:].astype(BF16)

    for load in loads:
        load.wait()
    for n in range(2):
        edge_copy(n).wait_recv()
    for m in range(2):
        low = lax.broadcasted_iota(jnp.int32, (128, size), 0) < 128 - lax.rem(row_ref[2, 0, 2 * m], 128)
        for part in range(2):
            cross[m, part] = jnp.where(
                low, edge[0, m, part].astype(F32), edge[1, m, part].astype(F32)).astype(BF16)
        either(is_self(2, m), lambda: cross_copy(m).start(), lambda: cross_here(m).start())

    @pl.when(active)
    def _():
        icopy.start()
        offset = lax.rem(row_ref[2, 0, 2 * half], 128)
        for big, big_t, src in ((big_m, big_mt, prop), (big_f, big_ft, table)):
            re, im = src[0], src[1]
            re_t, im_t = re.T, im.T
            big[:size, :size] = re
            big[:size, size:] = -im
            big[size:, :size] = im
            big[size:, size:] = re
            big_t[:size, :size] = re_t
            big_t[:size, size:] = im_t
            big_t[size:, :size] = -im_t
            big_t[size:, size:] = re_t
        head = lax.broadcasted_iota(jnp.int32, (128, size), 0) < 128 - offset

        def window_rows(s, part, e):
            top = win[s, part, e * 128:(e + 1) * 128, :].astype(F32)
            after = (e + 1) % 4
            low = win[s, part, after * 128:(after + 1) * 128, :].astype(F32)
            return jnp.where(head, top, low)

        def forward(s, carry):
            for e in range(4):
                same, here = None, None
                if e == 0:
                    same, here = cut == s, lambda: cross_here(half).wait()
                elif e == 2:
                    same, here = cut == s, lambda: window_here(half).wait()
                either(same, lambda: window_arrival(s, e).wait(), here)
            for e in range(4):
                rows = slice(e * 128, (e + 1) * 128)
                rows_im = slice(size + e * 128, size + (e + 1) * 128)
                w_re, w_im = window_rows(s, 0, e), window_rows(s, 1, e)
                p_re, p_im = waves[s, 0, rows].astype(F32), waves[s, 1, rows].astype(F32)
                upright[rows] = (p_re * w_re - p_im * w_im).astype(BF16)
                upright[rows_im] = (p_re * w_im + p_im * w_re).astype(BF16)
            left(big_m)
            made = dot(flat[...], big_mt[...])
            waves[s + 1, 0] = made[:, :size].astype(BF16)
            waves[s + 1, 1] = made[:, size:].astype(BF16)
            return carry
        lax.fori_loop(0, slices, forward, 0)

        upright[:size] = waves[slices, 0]
        upright[size:] = waves[slices, 1]
        left(big_f)
        icopy.wait()
        made = dot(flat[...], big_ft[...])
        for e in range(4):
            rows = slice(e * 128, (e + 1) * 128)
            re, im = made[rows, :size], made[rows, size:]
            excess = re * re + im * im - intensity[rows]
            upright[rows] = (excess * re).astype(BF16)
            upright[size + e * 128:size + (e + 1) * 128] = (excess * im).astype(BF16)
        left(big_ft)
        flat[...] = dot(flat[...], big_f[...]).astype(BF16)

        def backward(n, carry):
            s = slices - 1 - n
            made = dot(flat[...], big_m[...])
            upright[:size] = made[:, :size].astype(BF16)
            upright[size:] = made[:, size:].astype(BF16)
            made = dot(big_mt[...], upright[...])
            terms = []
            for e in range(4):
                rows = slice(e * 128, (e + 1) * 128)
                g_re, g_im = made[rows], made[size + e * 128:size + (e + 1) * 128]
                p_re, p_im = waves[s, 0, rows].astype(F32), waves[s, 1, rows].astype(F32)
                terms.append((p_re * g_re + p_im * g_im, p_re * g_im - p_im * g_re))
            for e in range(4):
                for part in range(2):
                    out[s, e, part] = jnp.where(head, terms[e][part], terms[e - 1][part]).astype(BF16)
            either(cut == s, lambda: back_copy(s).start(), lambda: back_here().start())
            for d in (1, 3, 2):
                either(cut == s if d == 2 else None,
                       lambda: block_copy(d, s).start(), lambda: block_here().start())
            for e in range(4):
                rows = slice(e * 128, (e + 1) * 128)
                g_re, g_im = made[rows], made[size + e * 128:size + (e + 1) * 128]
                w_re, w_im = window_rows(s, 0, e), window_rows(s, 1, e)
                flat[rows, :size] = (w_re * g_re + w_im * g_im).astype(BF16)
                flat[rows, size:] = (w_re * g_im - w_im * g_re).astype(BF16)
            return carry
        lax.fori_loop(0, slices, backward, 0)

    for m in range(2):
        either(is_self(2, m),
               lambda: pltpu.make_async_copy(out.at[0, 0], back.at[m], back_recv.at[m]).wait(),
               lambda: back_here().wait())
        for n in range(2):
            last_copy(m, n).start()

    for n in range(2):
        edge_copy(n).wait_send()
    for m in range(2):
        either(is_self(2, m), lambda: cross_copy(m).wait_send(), None)
        for d in (1, 2, 3):
            either(is_self(d, m), lambda: window_copy(d, m).wait_send(), None)

    @pl.when(active)
    def _():
        for k in range(4):
            either(cut == k, lambda: back_copy(k).wait_send(), None)
            for d in (1, 2, 3):
                either(cut == k if d == 2 else None,
                       lambda: block_copy(d, k).wait_send(), lambda: block_here().wait())

    for m in range(2):
        for d in range(REACH):
            either(is_self(d, m),
                   lambda: pltpu.make_async_copy(out.at[0, 0], got.at[d, m], out_recv.at[d, m]).wait(), None)
        for n in range(2):
            last_copy(m, n).wait_send()


def add_kernel(pos_ref, got_ref, out, acc, got, load_sem):
    width = out.shape[3]
    window = got.shape[4]
    loads = [pltpu.make_async_copy(got_ref.at[d], got.at[d], load_sem.at[d]) for d in range(REACH)]
    for load in loads:
        load.start()
    acc[...] = jnp.zeros_like(acc)
    row = 8 * lax.broadcasted_iota(jnp.int32, (16, 8, LANES), 0) + lax.broadcasted_iota(jnp.int32, (16, 8, LANES), 1)
    lane = lax.broadcasted_iota(jnp.int32, (16, 8, LANES), 2)
    sub = lax.broadcasted_iota(jnp.int32, (17, 8, LANES), 1)
    count = window // LANES
    zero = jnp.zeros((16, 8, LANES), F32)
    gap = jnp.zeros((1, 8, LANES), F32)
    for d in range(REACH):
        loads[d].wait()
        for m in range(2):
            offset = lax.rem(pos_ref[d, 0, 2 * m], 128)
            tile_row, low_row = offset // 8, lax.rem(offset, 8)
            base, shift = column_split(pos_ref[d, 0, 2 * m + 1], width, window)
            turn = lax.rem(shift, LANES)
            mine = None
            if d == 0:
                mine = row < 128 - offset
            elif d == REACH - 1:
                mine = row >= 128 - offset
            keep = lane >= shift
            keep_row = sub >= low_row
            to_rows = pl.ds(pl.multiple_of(tile_row * 8, 8), 136)
            for part in range(2):
                before = zero
                for j in range(count + 1):
                    here = zero
                    if j < count:
                        here = got[d, m, part, :, j * LANES:(j + 1) * LANES].astype(F32).reshape(16, 8, LANES)
                        if mine is not None:
                            here = jnp.where(mine, here, 0.0)
                        here = pltpu.roll(here, turn, 2)
                    moved = pltpu.roll(jnp.where(keep, here, before), low_row, 1)
                    before = here
                    made = jnp.where(keep_row, jnp.concatenate([moved, gap]), jnp.concatenate([gap, moved]))
                    to_cols = pl.ds(pl.multiple_of(base + j * LANES, LANES), LANES)
                    acc[part, to_rows, to_cols] += made.reshape(136, LANES)
    out[:, 0] = acc[:, :128] + acc[:, 128:]


def local(probe_wave, propagator, object_slices, positions, intensities):
    count = lax.axis_size("scan")
    size = probe_wave.shape[1]
    vmem = pl.BlockSpec(memory_space=pltpu.VMEM)
    smem = pl.BlockSpec(memory_space=pltpu.SMEM)
    anywhere = pl.BlockSpec(memory_space=pl.ANY)
    dma = pltpu.SemaphoreType.DMA
    pos = pl.pallas_call(
        functools.partial(positions_kernel, count),
        out_shape=jax.ShapeDtypeStruct((REACH, 8, LANES), jnp.int32),
        in_specs=[smem],
        out_specs=vmem,
        scratch_shapes=[
            pltpu.VMEM((8, LANES), jnp.int32), pltpu.VMEM((4, 8, LANES), jnp.int32), dma((4,)), dma((4,))],
        compiler_params=pltpu.CompilerParams(
            collective_id=0, has_side_effects=True, vmem_limit_bytes=4 * 2**20),
        name="share_positions",
    )(positions)

    stage = pl.pallas_call(
        pack_kernel,
        out_shape=jax.ShapeDtypeStruct((10, 2, 128, size), BF16),
        in_specs=[smem, anywhere],
        out_specs=vmem,
        scratch_shapes=[pltpu.VMEM((2, 256, object_slices.shape[3]), F32), dma((2,))],
        compiler_params=pltpu.CompilerParams(vmem_limit_bytes=24 * 2**20),
        name="pack_windows",
    )(pos, object_slices)

    got = pl.pallas_call(
        functools.partial(chain_kernel, count),
        out_shape=jax.ShapeDtypeStruct((REACH, 2, 2, 128, size), BF16),
        in_specs=[smem, vmem, anywhere, anywhere, anywhere, anywhere],
        out_specs=anywhere,
        scratch_shapes=[
            pltpu.VMEM((4, 2, size, size), BF16),
            pltpu.VMEM((size, size), F32),
            pltpu.VMEM((4, 4, 2, 128, size), BF16),
            pltpu.VMEM((2, 2, 2, 128, size), BF16),
            pltpu.VMEM((2, 2, 128, size), BF16),
            pltpu.VMEM((2, 2, 128, size), BF16),
            pltpu.VMEM((2, size, size), BF16),
            pltpu.VMEM((2, size, size), BF16),
        ]
        + [pltpu.VMEM((2 * size, 2 * size), BF16)] * 4
        + [
            pltpu.VMEM((2 * size, size), BF16),
            pltpu.VMEM((size, 2 * size), BF16),
            pltpu.VMEM((5, 2, size, size), BF16),
            dma((3,)), dma((10,)), dma((4, 4)), dma, dma((2,)), dma((2,)), dma((2,)), dma,
            dma, dma, dma((4, 4)), dma((REACH, 2)), dma, dma((4,)), dma((2,)), dma, dma((2, 2)),
        ],
        compiler_params=pltpu.CompilerParams(
            collective_id=1, has_side_effects=True, vmem_limit_bytes=52 * 2**20),
        name="chain",
    )(pos, stage, intensities, probe_wave, propagator, dft_table(size))

    return pl.pallas_call(
        add_kernel,
        out_shape=jax.ShapeDtypeStruct(object_slices.shape, F32),
        in_specs=[smem, anywhere],
        out_specs=vmem,
        scratch_shapes=[
            pltpu.VMEM((2, 256, object_slices.shape[3]), F32), pltpu.VMEM(got.shape, BF16), dma((REACH,))],
        compiler_params=pltpu.CompilerParams(vmem_limit_bytes=24 * 2**20),
        name="add_gradients",
    )(pos, got)


def solution(mesh):
    in_specs = (P(), P(), P(None, "cuts", "scan", None), P("scan", None), P("scan", None, None))
    out_specs = P(None, "cuts", "scan", None)
    return jax.shard_map(local, mesh=mesh, in_specs=in_specs, out_specs=out_specs, check_vma=False)
```

```python
import functools
import math

import jax
import jax.numpy as jnp
import numpy as np
from jax import lax
from jax.experimental import pallas as pl
from jax.experimental.pallas import tpu as pltpu
from jax.sharding import PartitionSpec as P

MESH = pl.DeviceIdType.MESH
BF16 = jnp.bfloat16
F32 = jnp.float32
REACH = 5
LANES = 128


def dft_table(length):
    serial = np.arange(length, dtype=np.int32)
    angle_index = serial[:, None] * serial[None, :] % length
    angle = angle_index.astype(np.float32) * np.float32(2.0 * math.pi / length)
    scale = np.float32(1.0 / math.sqrt(length))
    return jnp.asarray(
        np.stack([np.cos(angle) * scale, -np.sin(angle) * scale]), dtype=BF16
    )


def place():
    me = lax.axis_index("scan")
    cut = lax.axis_index("cuts")
    return me, cut, lax.rem(me, 2)


def wrapped(index, count):
    return lax.rem(index + 2 * count, count)


def worker(me, d, m, count):
    band = wrapped(me - d, count)
    return wrapped(me - d + 2, count), 2 * lax.rem(band, 2) + m


def column_split(column, width, window):
    base = jnp.minimum(column // LANES * LANES, width - window - LANES)
    return pl.multiple_of(base, LANES), column - base


def positions_kernel(count, pos_ref, band, pos_out, band2, pos_own, tile, pos_in, load_sem, psend, precv):
    me, cut, parity = place()
    loads = [pltpu.make_async_copy(pos_ref, pos_own, load_sem.at[2])] + [
        pltpu.make_async_copy(band.at[:, 0], band2.at[:, pl.ds(h * 128, 128), :], load_sem.at[h])
        for h in range(2)
    ]
    for load in loads:
        load.start()
    barrier = pltpu.get_barrier_semaphore()
    for d in range(1, REACH):
        pl.semaphore_signal(barrier, inc=1, device_id=(wrapped(me - d, count), cut), device_id_type=MESH)
    loads[0].wait()
    lane = lax.broadcasted_iota(jnp.int32, (8, LANES), 1)
    values = jnp.zeros((8, LANES), jnp.int32)
    for n in range(4):
        values = jnp.where(lane == n, pos_own[n // 2, n % 2], values)
    tile[...] = values
    pos_out[...] = values
    pl.semaphore_wait(barrier, REACH - 1)
    copies = []
    for d in range(1, REACH):
        copy = pltpu.make_async_remote_copy(
            src_ref=tile, dst_ref=pos_in.at[d - 1], send_sem=psend.at[d - 1], recv_sem=precv.at[d - 1],
            device_id=(wrapped(me + d, count), cut), device_id_type=MESH)
        copy.start()
        copies.append(copy)
    for d in range(1, REACH):
        copies[d - 1].wait()
        pos_out[d:d + 1] = pos_in[d - 1, 0:1]
    for load in loads[1:]:
        load.wait()


def pack_kernel(pos_ref, band2, stage):
    window = stage.shape[3]
    width = band2.shape[2]
    lane = lax.broadcasted_iota(jnp.int32, (17, 8, LANES), 2)
    sub = lax.broadcasted_iota(jnp.int32, (16, 8, LANES), 1)
    for d in range(REACH):
        for m in range(2):
            offset = lax.rem(pos_ref[d, 2 * m], 128)
            tile_row, low_row = offset // 8, lax.rem(offset, 8)
            base, shift = column_split(pos_ref[d, 2 * m + 1], width, window)
            turn = lax.rem(LANES - shift, LANES)
            lift = lax.rem(8 - low_row, 8)
            keep = lane + shift < LANES
            keep_row = sub + low_row < 8
            rows = pl.ds(pl.multiple_of(tile_row * 8, 8), 136)
            for part in range(2):
                turned = []
                for j in range(window // LANES + 1):
                    cols = pl.ds(pl.multiple_of(base + j * LANES, LANES), LANES)
                    turned.append(pltpu.roll(band2[part, rows, cols].reshape(17, 8, LANES), turn, 2))
                for j in range(window // LANES):
                    lifted = pltpu.roll(jnp.where(keep, turned[j], turned[j + 1]), lift, 1)
                    made = jnp.where(keep_row, lifted[:16], lifted[1:]).reshape(128, LANES)
                    stage[d * 2 + m, part, :, j * LANES:(j + 1) * LANES] = made.astype(BF16)


def chain_kernel(count, row_ref, stage, int_ref, probe_ref, prop_ref, table_ref, got,
                 win, intensity, out, edge, cross, back, prop, table,
                 bigs, bigs_t, upright, flat, waves,
                 load_sem, win_send, win_recv, self_sem, edge_send, edge_recv, cross_send, cross_self,
                 isend, irecv, out_send, out_recv, out_self, back_send, back_recv, back_self, last_send):
    me, cut, parity = place()
    size = flat.shape[0]
    slices = win.shape[0]
    active = (cut // 2) == parity
    half = lax.rem(cut, 2)
    behind, ahead = wrapped(me - 2, count), wrapped(me + 2, count)

    def owner(d, k):
        return wrapped(me - 2 + d, count), jnp.int32(k)

    def is_self(d, m):
        return cut == 2 * parity + m if d == 2 else None

    def either(same, remote, here):
        if same is None:
            remote()
        else:
            pl.when(jnp.logical_not(same))(remote)
            if here is not None:
                pl.when(same)(here)

    loads = [
        pltpu.make_async_copy(src, dst, load_sem.at[n])
        for n, (src, dst) in enumerate(((probe_ref, waves.at[0]), (prop_ref, prop), (table_ref, table)))
    ]
    for load in loads:
        load.start()

    barrier = pltpu.get_barrier_semaphore()

    def greet(device):
        pl.semaphore_signal(barrier, inc=1, device_id=device, device_id_type=MESH)

    greet((behind, cut))
    greet((ahead, cut))
    for m in range(2):
        for d in (1, 2, 3):
            either(is_self(d, m), lambda: greet(worker(me, d, m, count)), None)
        either(is_self(2, m), lambda: greet(worker(me, 2, m, count)), None)

    @pl.when(active)
    def _():
        for k in range(4):
            for d in (1, 2, 3):
                either(cut == k if d == 2 else None, lambda: greet(owner(d, k)), None)
            either(cut == k, lambda: greet(owner(2, k)), None)

    pl.semaphore_wait(barrier, jnp.where(active, 22, 10))

    def unit(s, e):
        return win.at[s, :, pl.ds(e * 128, 128), :]

    def window_copy(d, m):
        return pltpu.make_async_remote_copy(
            src_ref=stage.at[d * 2 + m], dst_ref=unit(cut, d),
            send_sem=win_send.at[d * 2 + m], recv_sem=win_recv.at[cut, d],
            device_id=worker(me, d, m, count), device_id_type=MESH)

    def window_here(m):
        return pltpu.make_async_copy(stage.at[4 + m], unit(cut, 2), self_sem)

    def edge_copy(n):
        return pltpu.make_async_remote_copy(
            src_ref=stage.at[pl.ds(8 * n, 2)], dst_ref=edge.at[n],
            send_sem=edge_send.at[n], recv_sem=edge_recv.at[n],
            device_id=((ahead, behind)[n], cut), device_id_type=MESH)

    def cross_copy(m):
        return pltpu.make_async_remote_copy(
            src_ref=cross.at[m], dst_ref=unit(cut, 0), send_sem=cross_send.at[m], recv_sem=win_recv.at[cut, 0],
            device_id=(me, 2 * parity + m), device_id_type=MESH)

    def cross_here(m):
        return pltpu.make_async_copy(cross.at[m], unit(cut, 0), cross_self)

    def window_arrival(s, e):
        return pltpu.make_async_copy(stage.at[0], unit(s, e), win_recv.at[s, e])

    def block_copy(d, k):
        return pltpu.make_async_remote_copy(
            src_ref=out.at[k, d], dst_ref=got.at[d, half],
            send_sem=out_send.at[k, d], recv_sem=out_recv.at[d, half],
            device_id=owner(d, k), device_id_type=MESH)

    def block_here():
        return pltpu.make_async_copy(out.at[cut, 2], got.at[2, half], out_self)

    def back_copy(k):
        return pltpu.make_async_remote_copy(
            src_ref=out.at[k, 0], dst_ref=back.at[half], send_sem=back_send.at[k], recv_sem=back_recv.at[half],
            device_id=(me, jnp.int32(k)), device_id_type=MESH)

    def back_here():
        return pltpu.make_async_copy(out.at[cut, 0], back.at[half], back_self)

    def last_copy(m, n):
        return pltpu.make_async_remote_copy(
            src_ref=back.at[m], dst_ref=got.at[4 * n, m], send_sem=last_send.at[m, n], recv_sem=out_recv.at[4 * n, m],
            device_id=((behind, ahead)[n], cut), device_id_type=MESH)

    icopy = pltpu.make_async_remote_copy(
        src_ref=int_ref.at[half], dst_ref=intensity, send_sem=isend, recv_sem=irecv,
        device_id=(ahead, cut), device_id_type=MESH)

    for n in range(2):
        edge_copy(n).start()
    for d in (1, 3, 2):
        for m in range(2):
            either(is_self(d, m), lambda: window_copy(d, m).start(), lambda: window_here(m).start())

    def dot(a, b):
        return jnp.dot(a, b, preferred_element_type=F32)

    def left(big):
        made = dot(big[...], upright[...])
        flat[:, :size] = made[:size].astype(BF16)
        flat[:, size:] = made[size:].astype(BF16)

    for load in loads:
        load.wait()

    def spread_out(big, re, im):
        big[:size, :size] = re
        big[:size, size:] = -im
        big[size:, :size] = im
        big[size:, size:] = re

    @pl.when(active)
    def _():
        icopy.start()
        upright[:size] = prop[0]
        upright[size:] = prop[1]
        spread_out(bigs.at[0], prop[0], prop[1])
        spread_out(bigs_t.at[0], prop[0].T, -prop[1].T)
        spread_out(bigs_t.at[1], table[0], table[1])
        made = dot(bigs_t[1], upright[...]).astype(BF16)
        spread_out(bigs.at[1], made[:size], made[size:])
        spread_out(bigs_t.at[1], made[:size].T, -made[size:].T)

    for n in range(2):
        edge_copy(n).wait_recv()
    for m in range(2):
        low = lax.broadcasted_iota(jnp.int32, (128, size), 0) < 128 - lax.rem(row_ref[2, 2 * m], 128)
        for part in range(2):
            cross[m, part] = jnp.where(
                low, edge[0, m, part].astype(F32), edge[1, m, part].astype(F32)).astype(BF16)
        either(is_self(2, m), lambda: cross_copy(m).start(), lambda: cross_here(m).start())

    @pl.when(active)
    def _():
        offset = lax.rem(row_ref[2, 2 * half], 128)
        head = lax.broadcasted_iota(jnp.int32, (128, size), 0) < 128 - offset

        def window_rows(s, part, e):
            top = win[s, part, e * 128:(e + 1) * 128, :].astype(F32)
            after = (e + 1) % 4
            low = win[s, part, after * 128:(after + 1) * 128, :].astype(F32)
            return jnp.where(head, top, low)

        def enter(s):
            for e in range(4):
                same, here = None, None
                if e == 0:
                    same, here = cut == s, lambda: cross_here(half).wait()
                elif e == 2:
                    same, here = cut == s, lambda: window_here(half).wait()
                either(same, lambda: window_arrival(s, e).wait(), here)
            for e in range(4):
                rows = slice(e * 128, (e + 1) * 128)
                rows_im = slice(size + e * 128, size + (e + 1) * 128)
                w_re, w_im = window_rows(s, 0, e), window_rows(s, 1, e)
                p_re, p_im = waves[s, 0, rows].astype(F32), waves[s, 1, rows].astype(F32)
                upright[rows] = (p_re * w_re - p_im * w_im).astype(BF16)
                upright[rows_im] = (p_re * w_im + p_im * w_re).astype(BF16)

        def forward(s, carry):
            enter(s)
            left(bigs.at[0])
            made = dot(flat[...], bigs_t[0])
            waves[s + 1, 0] = made[:, :size].astype(BF16)
            waves[s + 1, 1] = made[:, size:].astype(BF16)
            return carry
        lax.fori_loop(0, slices - 1, forward, 0)

        enter(slices - 1)
        left(bigs.at[1])
        icopy.wait()
        made = dot(flat[...], bigs_t[1])
        for e in range(4):
            rows = slice(e * 128, (e + 1) * 128)
            re, im = made[rows, :size], made[rows, size:]
            excess = re * re + im * im - intensity[rows]
            flat[rows, :size] = (excess * re).astype(BF16)
            flat[rows, size:] = (excess * im).astype(BF16)

        def backward(n, carry):
            s = slices - 1 - n
            which = jnp.where(n == 0, 1, 0)
            made = dot(flat[...], bigs[which])
            upright[:size] = made[:, :size].astype(BF16)
            upright[size:] = made[:, size:].astype(BF16)
            made = dot(bigs_t[which], upright[...])
            terms = []
            for e in range(4):
                rows = slice(e * 128, (e + 1) * 128)
                g_re, g_im = made[rows], made[size + e * 128:size + (e + 1) * 128]
                p_re, p_im = waves[s, 0, rows].astype(F32), waves[s, 1, rows].astype(F32)
                terms.append((p_re * g_re + p_im * g_im, p_re * g_im - p_im * g_re))
            for e in range(4):
                for part in range(2):
                    out[s, e, part] = jnp.where(head, terms[e][part], terms[e - 1][part]).astype(BF16)
            either(cut == s, lambda: back_copy(s).start(), lambda: back_here().start())
            for d in (1, 3, 2):
                either(cut == s if d == 2 else None,
                       lambda: block_copy(d, s).start(), lambda: block_here().start())
            for e in range(4):
                rows = slice(e * 128, (e + 1) * 128)
                g_re, g_im = made[rows], made[size + e * 128:size + (e + 1) * 128]
                w_re, w_im = window_rows(s, 0, e), window_rows(s, 1, e)
                flat[rows, :size] = (w_re * g_re + w_im * g_im).astype(BF16)
                flat[rows, size:] = (w_re * g_im - w_im * g_re).astype(BF16)
            return carry
        lax.fori_loop(0, slices, backward, 0)

    for m in range(2):
        either(is_self(2, m),
               lambda: pltpu.make_async_copy(out.at[0, 0], back.at[m], back_recv.at[m]).wait(),
               lambda: back_here().wait())
        for n in range(2):
            last_copy(m, n).start()

    for n in range(2):
        edge_copy(n).wait_send()
    for m in range(2):
        either(is_self(2, m), lambda: cross_copy(m).wait_send(), None)
        for d in (1, 2, 3):
            either(is_self(d, m), lambda: window_copy(d, m).wait_send(), None)

    @pl.when(active)
    def _():
        for k in range(4):
            either(cut == k, lambda: back_copy(k).wait_send(), None)
            for d in (1, 2, 3):
                either(cut == k if d == 2 else None,
                       lambda: block_copy(d, k).wait_send(), lambda: block_here().wait())

    for m in range(2):
        for d in range(REACH):
            either(is_self(d, m),
                   lambda: pltpu.make_async_copy(out.at[0, 0], got.at[d, m], out_recv.at[d, m]).wait(), None)
        for n in range(2):
            last_copy(m, n).wait_send()


def add_kernel(pos_ref, got, out, acc):
    width = out.shape[3]
    window = got.shape[4]
    acc[...] = jnp.zeros_like(acc)
    row = 8 * lax.broadcasted_iota(jnp.int32, (16, 8, LANES), 0) + lax.broadcasted_iota(jnp.int32, (16, 8, LANES), 1)
    lane = lax.broadcasted_iota(jnp.int32, (16, 8, LANES), 2)
    sub = lax.broadcasted_iota(jnp.int32, (17, 8, LANES), 1)
    count = window // LANES
    zero = jnp.zeros((16, 8, LANES), F32)
    gap = jnp.zeros((1, 8, LANES), F32)
    for d in range(REACH):
        for m in range(2):
            offset = lax.rem(pos_ref[d, 2 * m], 128)
            tile_row, low_row = offset // 8, lax.rem(offset, 8)
            base, shift = column_split(pos_ref[d, 2 * m + 1], width, window)
            turn = lax.rem(shift, LANES)
            mine = None
            if d == 0:
                mine = row < 128 - offset
            elif d == REACH - 1:
                mine = row >= 128 - offset
            keep = lane >= shift
            keep_row = sub >= low_row
            to_rows = pl.ds(pl.multiple_of(tile_row * 8, 8), 136)
            for part in range(2):
                before = zero
                for j in range(count + 1):
                    here = zero
                    if j < count:
                        here = got[d, m, part, :, j * LANES:(j + 1) * LANES].astype(F32).reshape(16, 8, LANES)
                        if mine is not None:
                            here = jnp.where(mine, here, 0.0)
                        here = pltpu.roll(here, turn, 2)
                    moved = pltpu.roll(jnp.where(keep, here, before), low_row, 1)
                    before = here
                    made = jnp.where(keep_row, jnp.concatenate([moved, gap]), jnp.concatenate([gap, moved]))
                    to_cols = pl.ds(pl.multiple_of(base + j * LANES, LANES), LANES)
                    acc[part, to_rows, to_cols] += made.reshape(136, LANES)
    out[:, 0] = acc[:, :128] + acc[:, 128:]


def local(probe_wave, propagator, object_slices, positions, intensities):
    count = lax.axis_size("scan")
    size = probe_wave.shape[1]
    vmem = pl.BlockSpec(memory_space=pltpu.VMEM)
    smem = pl.BlockSpec(memory_space=pltpu.SMEM)
    anywhere = pl.BlockSpec(memory_space=pl.ANY)
    hbm = pl.BlockSpec(memory_space=pltpu.HBM)
    dma = pltpu.SemaphoreType.DMA
    pos, band2 = pl.pallas_call(
        functools.partial(positions_kernel, count),
        out_shape=[
            jax.ShapeDtypeStruct((8, LANES), jnp.int32),
            jax.ShapeDtypeStruct((2, 256, object_slices.shape[3]), F32),
        ],
        in_specs=[hbm, hbm],
        out_specs=[vmem, vmem],
        scratch_shapes=[
            pltpu.SMEM((2, 2), jnp.int32), pltpu.VMEM((8, LANES), jnp.int32), pltpu.VMEM((4, 8, LANES), jnp.int32),
            dma((3,)), dma((4,)), dma((4,))],
        compiler_params=pltpu.CompilerParams(
            collective_id=0, has_side_effects=True, vmem_limit_bytes=16 * 2**20),
        name="share_positions",
    )(positions, object_slices)

    stage = pl.pallas_call(
        pack_kernel,
        out_shape=jax.ShapeDtypeStruct((10, 2, 128, size), BF16),
        in_specs=[smem, vmem],
        out_specs=vmem,
        compiler_params=pltpu.CompilerParams(vmem_limit_bytes=24 * 2**20),
        name="pack_windows",
    )(pos, band2)

    got = pl.pallas_call(
        functools.partial(chain_kernel, count),
        out_shape=jax.ShapeDtypeStruct((REACH, 2, 2, 128, size), BF16),
        in_specs=[smem, vmem, hbm, hbm, hbm, hbm],
        out_specs=vmem,
        scratch_shapes=[
            pltpu.VMEM((4, 2, size, size), BF16),
            pltpu.VMEM((size, size), F32),
            pltpu.VMEM((4, 4, 2, 128, size), BF16),
            pltpu.VMEM((2, 2, 2, 128, size), BF16),
            pltpu.VMEM((2, 2, 128, size), BF16),
            pltpu.VMEM((2, 2, 128, size), BF16),
            pltpu.VMEM((2, size, size), BF16),
            pltpu.VMEM((2, size, size), BF16),
        ]
        + [pltpu.VMEM((2, 2 * size, 2 * size), BF16)] * 2
        + [
            pltpu.VMEM((2 * size, size), BF16),
            pltpu.VMEM((size, 2 * size), BF16),
            pltpu.VMEM((4, 2, size, size), BF16),
            dma((3,)), dma((10,)), dma((4, 4)), dma, dma((2,)), dma((2,)), dma((2,)), dma,
            dma, dma, dma((4, 4)), dma((REACH, 2)), dma, dma((4,)), dma((2,)), dma, dma((2, 2)),
        ],
        compiler_params=pltpu.CompilerParams(
            collective_id=1, has_side_effects=True, vmem_limit_bytes=40 * 2**20),
        name="chain",
    )(pos, stage, intensities, probe_wave, propagator, dft_table(size))

    return pl.pallas_call(
        add_kernel,
        out_shape=jax.ShapeDtypeStruct(object_slices.shape, F32),
        in_specs=[smem, vmem],
        out_specs=vmem,
        scratch_shapes=[pltpu.VMEM((2, 256, object_slices.shape[3]), F32)],
        compiler_params=pltpu.CompilerParams(vmem_limit_bytes=24 * 2**20),
        name="add_gradients",
    )(pos, got)


def solution(mesh):
    in_specs = (P(), P(), P(None, "cuts", "scan", None), P("scan", None), P("scan", None, None))
    out_specs = P(None, "cuts", "scan", None)
    return jax.shard_map(local, mesh=mesh, in_specs=in_specs, out_specs=out_specs, check_vma=False)
```

```python
import functools
import math

import jax
import jax.numpy as jnp
import numpy as np
from jax import lax
from jax.experimental import pallas as pl
from jax.experimental.pallas import tpu as pltpu
from jax.sharding import PartitionSpec as P

MESH = pl.DeviceIdType.MESH
BF16 = jnp.bfloat16
F32 = jnp.float32
REACH = 5
LANES = 128


def dft_table(length):
    serial = np.arange(length, dtype=np.int32)
    angle_index = serial[:, None] * serial[None, :] % length
    angle = angle_index.astype(np.float32) * np.float32(2.0 * math.pi / length)
    scale = np.float32(1.0 / math.sqrt(length))
    return jnp.asarray(
        np.stack([np.cos(angle) * scale, -np.sin(angle) * scale]), dtype=BF16
    )


def place():
    me = lax.axis_index("scan")
    cut = lax.axis_index("cuts")
    return me, cut, lax.rem(me, 2)


def wrapped(index, count):
    return lax.rem(index + 2 * count, count)


def worker(me, d, m, count):
    band = wrapped(me - d, count)
    return wrapped(me - d + 2, count), 2 * lax.rem(band, 2) + m


def column_split(column, width, window):
    base = jnp.minimum(column // LANES * LANES, width - window - LANES)
    return pl.multiple_of(base, LANES), column - base


def positions_kernel(count, pos_ref, band, pos_out, tiles, pos_own, tile, pos_in, load_sem, band_sem, psend, precv):
    me, cut, parity = place()
    loads = [pltpu.make_async_copy(pos_ref, pos_own, load_sem)] + [
        pltpu.make_async_copy(
            band.at[part, :, :, pl.ds(n * LANES, LANES)], tiles.at[part, n], band_sem.at[part, n])
        for part in range(2)
        for n in range(tiles.shape[1])
    ]
    for load in loads:
        load.start()
    barrier = pltpu.get_barrier_semaphore()
    for d in range(1, REACH):
        pl.semaphore_signal(barrier, inc=1, device_id=(wrapped(me - d, count), cut), device_id_type=MESH)
    loads[0].wait()
    lane = lax.broadcasted_iota(jnp.int32, (8, LANES), 1)
    values = jnp.zeros((8, LANES), jnp.int32)
    for n in range(4):
        values = jnp.where(lane == n, pos_own[n // 2, n % 2], values)
    tile[...] = values
    pos_out[...] = values
    pl.semaphore_wait(barrier, REACH - 1)
    copies = []
    for d in range(1, REACH):
        copy = pltpu.make_async_remote_copy(
            src_ref=tile, dst_ref=pos_in.at[d - 1], send_sem=psend.at[d - 1], recv_sem=precv.at[d - 1],
            device_id=(wrapped(me + d, count), cut), device_id_type=MESH)
        copy.start()
        copies.append(copy)
    for d in range(1, REACH):
        copies[d - 1].wait()
        pos_out[d:d + 1] = pos_in[d - 1, 0:1]
    for load in loads[1:]:
        load.wait()


def pack(stage, tiles, slot, row, column):
    window, width = stage.shape[3], tiles.shape[1] * LANES
    lane = lax.broadcasted_iota(jnp.int32, (16, 8, LANES), 2)
    sub = lax.broadcasted_iota(jnp.int32, (16, 8, LANES), 1)
    offset = lax.rem(row, 128)
    tile_row, low_row = offset // 8, lax.rem(offset, 8)
    tile_column = jnp.minimum(column // LANES, (width - window) // LANES - 1)
    shift = column - tile_column * LANES
    turn = lax.rem(LANES - shift, LANES)
    lift = lax.rem(8 - low_row, 8)
    keep = lane + shift < LANES
    keep_row = sub + low_row < 8
    rows = [lax.rem(tile_row + t, 16) for t in range(16)]

    def one_part(part, carry):
        turned = []
        for j in range(window // LANES + 1):
            turned.append(pltpu.roll(
                jnp.stack([tiles[part, tile_column + j, rows[t]] for t in range(16)]), turn, 2))
        for j in range(window // LANES):
            lifted = pltpu.roll(jnp.where(keep, turned[j], turned[j + 1]), lift, 1)
            made = jnp.where(keep_row, lifted, jnp.concatenate([lifted[1:], lifted[:1]]))
            stage[slot, part, :, j * LANES:(j + 1) * LANES] = made.reshape(128, LANES).astype(BF16)
        return carry
    lax.fori_loop(0, 2, one_part, 0)


def chain_kernel(count, row_ref, tiles, int_ref, probe_ref, prop_ref, table_ref, got,
                 stage, win, intensity, out, edge, cross, back, prop, table,
                 bigs, bigs_t, upright, flat, waves,
                 load_sem, win_send, win_recv, self_sem, edge_send, edge_recv, cross_send, cross_self,
                 isend, irecv, out_send, out_recv, out_self, back_send, back_recv, back_self, last_send):
    me, cut, parity = place()
    size = flat.shape[0]
    slices = win.shape[0]
    active = (cut // 2) == parity
    half = lax.rem(cut, 2)
    behind, ahead = wrapped(me - 2, count), wrapped(me + 2, count)

    def owner(d, k):
        return wrapped(me - 2 + d, count), jnp.int32(k)

    def is_self(d, m):
        return cut == 2 * parity + m if d == 2 else None

    def either(same, remote, here):
        if same is None:
            remote()
        else:
            pl.when(jnp.logical_not(same))(remote)
            if here is not None:
                pl.when(same)(here)

    loads = [
        pltpu.make_async_copy(src, dst, load_sem.at[n])
        for n, (src, dst) in enumerate(((probe_ref, waves.at[0]), (prop_ref, prop), (table_ref, table)))
    ]
    for load in loads:
        load.start()

    barrier = pltpu.get_barrier_semaphore()

    def greet(device):
        pl.semaphore_signal(barrier, inc=1, device_id=device, device_id_type=MESH)

    greet((behind, cut))
    greet((ahead, cut))
    for m in range(2):
        for d in (1, 2, 3):
            either(is_self(d, m), lambda: greet(worker(me, d, m, count)), None)
        either(is_self(2, m), lambda: greet(worker(me, 2, m, count)), None)

    @pl.when(active)
    def _():
        for k in range(4):
            for d in (1, 2, 3):
                either(cut == k if d == 2 else None, lambda: greet(owner(d, k)), None)
            either(cut == k, lambda: greet(owner(2, k)), None)

    def pack_all(d):
        for m in range(2):
            pack(stage, tiles, d * 2 + m, row_ref[d, 2 * m], row_ref[d, 2 * m + 1])

    pack_all(0)
    pack_all(4)
    pl.semaphore_wait(barrier, jnp.where(active, 22, 10))

    def unit(s, e):
        return win.at[s, :, pl.ds(e * 128, 128), :]

    def window_copy(d, m):
        return pltpu.make_async_remote_copy(
            src_ref=stage.at[d * 2 + m], dst_ref=unit(cut, d),
            send_sem=win_send.at[d * 2 + m], recv_sem=win_recv.at[cut, d],
            device_id=worker(me, d, m, count), device_id_type=MESH)

    def window_here(m):
        return pltpu.make_async_copy(stage.at[4 + m], unit(cut, 2), self_sem)

    def edge_copy(n):
        return pltpu.make_async_remote_copy(
            src_ref=stage.at[pl.ds(8 * n, 2)], dst_ref=edge.at[n],
            send_sem=edge_send.at[n], recv_sem=edge_recv.at[n],
            device_id=((ahead, behind)[n], cut), device_id_type=MESH)

    def cross_copy(m):
        return pltpu.make_async_remote_copy(
            src_ref=cross.at[m], dst_ref=unit(cut, 0), send_sem=cross_send.at[m], recv_sem=win_recv.at[cut, 0],
            device_id=(me, 2 * parity + m), device_id_type=MESH)

    def cross_here(m):
        return pltpu.make_async_copy(cross.at[m], unit(cut, 0), cross_self)

    def window_arrival(s, e):
        return pltpu.make_async_copy(stage.at[0], unit(s, e), win_recv.at[s, e])

    def block_copy(d, k):
        return pltpu.make_async_remote_copy(
            src_ref=out.at[k, d], dst_ref=got.at[d, half],
            send_sem=out_send.at[k, d], recv_sem=out_recv.at[d, half],
            device_id=owner(d, k), device_id_type=MESH)

    def block_here():
        return pltpu.make_async_copy(out.at[cut, 2], got.at[2, half], out_self)

    def back_copy(k):
        return pltpu.make_async_remote_copy(
            src_ref=out.at[k, 0], dst_ref=back.at[half], send_sem=back_send.at[k], recv_sem=back_recv.at[half],
            device_id=(me, jnp.int32(k)), device_id_type=MESH)

    def back_here():
        return pltpu.make_async_copy(out.at[cut, 0], back.at[half], back_self)

    def last_copy(m, n):
        return pltpu.make_async_remote_copy(
            src_ref=back.at[m], dst_ref=got.at[4 * n, m], send_sem=last_send.at[m, n], recv_sem=out_recv.at[4 * n, m],
            device_id=((behind, ahead)[n], cut), device_id_type=MESH)

    icopy = pltpu.make_async_remote_copy(
        src_ref=int_ref.at[half], dst_ref=intensity, send_sem=isend, recv_sem=irecv,
        device_id=(ahead, cut), device_id_type=MESH)

    for n in range(2):
        edge_copy(n).start()
    for d in (1, 3, 2):
        pack_all(d)
        for m in range(2):
            either(is_self(d, m), lambda: window_copy(d, m).start(), lambda: window_here(m).start())

    def dot(a, b):
        return jnp.dot(a, b, preferred_element_type=F32)

    def left(big):
        made = dot(big[...], upright[...])
        flat[:, :size] = made[:size].astype(BF16)
        flat[:, size:] = made[size:].astype(BF16)

    for load in loads:
        load.wait()

    def spread_out(big, re, im):
        big[:size, :size] = re
        big[:size, size:] = -im
        big[size:, :size] = im
        big[size:, size:] = re

    @pl.when(active)
    def _():
        icopy.start()
        upright[:size] = prop[0]
        upright[size:] = prop[1]
        spread_out(bigs.at[0], prop[0], prop[1])
        spread_out(bigs_t.at[0], prop[0].T, -prop[1].T)
        spread_out(bigs_t.at[1], table[0], table[1])
        made = dot(bigs_t[1], upright[...]).astype(BF16)
        spread_out(bigs.at[1], made[:size], made[size:])
        spread_out(bigs_t.at[1], made[:size].T, -made[size:].T)

    for n in range(2):
        edge_copy(n).wait_recv()
    for m in range(2):
        low = lax.broadcasted_iota(jnp.int32, (128, size), 0) < 128 - lax.rem(row_ref[2, 2 * m], 128)
        for part in range(2):
            cross[m, part] = jnp.where(
                low, edge[0, m, part].astype(F32), edge[1, m, part].astype(F32)).astype(BF16)
        either(is_self(2, m), lambda: cross_copy(m).start(), lambda: cross_here(m).start())

    @pl.when(active)
    def _():
        offset = lax.rem(row_ref[2, 2 * half], 128)
        head = lax.broadcasted_iota(jnp.int32, (128, size), 0) < 128 - offset

        def window_rows(s, part, e):
            top = win[s, part, e * 128:(e + 1) * 128, :].astype(F32)
            after = (e + 1) % 4
            low = win[s, part, after * 128:(after + 1) * 128, :].astype(F32)
            return jnp.where(head, top, low)

        def enter(s):
            for e in range(4):
                same, here = None, None
                if e == 0:
                    same, here = cut == s, lambda: cross_here(half).wait()
                elif e == 2:
                    same, here = cut == s, lambda: window_here(half).wait()
                either(same, lambda: window_arrival(s, e).wait(), here)
            for e in range(4):
                rows = slice(e * 128, (e + 1) * 128)
                rows_im = slice(size + e * 128, size + (e + 1) * 128)
                w_re, w_im = window_rows(s, 0, e), window_rows(s, 1, e)
                p_re, p_im = waves[s, 0, rows].astype(F32), waves[s, 1, rows].astype(F32)
                upright[rows] = (p_re * w_re - p_im * w_im).astype(BF16)
                upright[rows_im] = (p_re * w_im + p_im * w_re).astype(BF16)

        def forward(s, carry):
            enter(s)
            left(bigs.at[0])
            made = dot(flat[...], bigs_t[0])
            waves[s + 1, 0] = made[:, :size].astype(BF16)
            waves[s + 1, 1] = made[:, size:].astype(BF16)
            return carry
        lax.fori_loop(0, slices - 1, forward, 0)

        enter(slices - 1)
        left(bigs.at[1])
        icopy.wait()
        made = dot(flat[...], bigs_t[1])
        for e in range(4):
            rows = slice(e * 128, (e + 1) * 128)
            re, im = made[rows, :size], made[rows, size:]
            excess = re * re + im * im - intensity[rows]
            flat[rows, :size] = (excess * re).astype(BF16)
            flat[rows, size:] = (excess * im).astype(BF16)

        def backward(n, carry):
            s = slices - 1 - n
            which = jnp.where(n == 0, 1, 0)
            made = dot(flat[...], bigs[which])
            upright[:size] = made[:, :size].astype(BF16)
            upright[size:] = made[:, size:].astype(BF16)
            made = dot(bigs_t[which], upright[...])
            terms = []
            for e in range(4):
                rows = slice(e * 128, (e + 1) * 128)
                g_re, g_im = made[rows], made[size + e * 128:size + (e + 1) * 128]
                p_re, p_im = waves[s, 0, rows].astype(F32), waves[s, 1, rows].astype(F32)
                terms.append((p_re * g_re + p_im * g_im, p_re * g_im - p_im * g_re))
            for e in range(4):
                for part in range(2):
                    out[s, e, part] = jnp.where(head, terms[e][part], terms[e - 1][part]).astype(BF16)
            either(cut == s, lambda: back_copy(s).start(), lambda: back_here().start())
            for d in (1, 3, 2):
                either(cut == s if d == 2 else None,
                       lambda: block_copy(d, s).start(), lambda: block_here().start())
            for e in range(4):
                rows = slice(e * 128, (e + 1) * 128)
                g_re, g_im = made[rows], made[size + e * 128:size + (e + 1) * 128]
                w_re, w_im = window_rows(s, 0, e), window_rows(s, 1, e)
                flat[rows, :size] = (w_re * g_re + w_im * g_im).astype(BF16)
                flat[rows, size:] = (w_re * g_im - w_im * g_re).astype(BF16)
            return carry
        lax.fori_loop(0, slices, backward, 0)

    for m in range(2):
        either(is_self(2, m),
               lambda: pltpu.make_async_copy(out.at[0, 0], back.at[m], back_recv.at[m]).wait(),
               lambda: back_here().wait())
        for n in range(2):
            last_copy(m, n).start()

    for n in range(2):
        edge_copy(n).wait_send()
    for m in range(2):
        either(is_self(2, m), lambda: cross_copy(m).wait_send(), None)
        for d in (1, 2, 3):
            either(is_self(d, m), lambda: window_copy(d, m).wait_send(), None)

    @pl.when(active)
    def _():
        for k in range(4):
            either(cut == k, lambda: back_copy(k).wait_send(), None)
            for d in (1, 2, 3):
                either(cut == k if d == 2 else None,
                       lambda: block_copy(d, k).wait_send(), lambda: block_here().wait())

    for m in range(2):
        for d in range(REACH):
            either(is_self(d, m),
                   lambda: pltpu.make_async_copy(out.at[0, 0], got.at[d, m], out_recv.at[d, m]).wait(), None)
        for n in range(2):
            last_copy(m, n).wait_send()


def add_kernel(pos_ref, got, out):
    width = out.shape[3]
    window = got.shape[4]
    out[...] = jnp.zeros_like(out)
    row = 8 * lax.broadcasted_iota(jnp.int32, (16, 8, LANES), 0) + lax.broadcasted_iota(jnp.int32, (16, 8, LANES), 1)
    lane = lax.broadcasted_iota(jnp.int32, (16, 8, LANES), 2)
    sub = lax.broadcasted_iota(jnp.int32, (16, 8, LANES), 1)
    count = window // LANES
    zero = jnp.zeros((16, 8, LANES), F32)
    for d in range(REACH):
        for m in range(2):
            offset = lax.rem(pos_ref[d, 2 * m], 128)
            tile_row, low_row = offset // 8, lax.rem(offset, 8)
            base, shift = column_split(pos_ref[d, 2 * m + 1], width, window)
            turn = lax.rem(shift, LANES)
            mine = None
            if d == 0:
                mine = row < 128 - offset
            elif d == REACH - 1:
                mine = row >= 128 - offset
            keep = lane >= shift
            keep_row = sub >= low_row
            to_rows = [pl.ds(pl.multiple_of(lax.rem(tile_row + t, 16) * 8, 8), 8) for t in range(16)]
            for part in range(2):
                before = zero
                for j in range(count + 1):
                    here = zero
                    if j < count:
                        here = got[d, m, part, :, j * LANES:(j + 1) * LANES].astype(F32).reshape(16, 8, LANES)
                        if mine is not None:
                            here = jnp.where(mine, here, 0.0)
                        here = pltpu.roll(here, turn, 2)
                    moved = pltpu.roll(jnp.where(keep, here, before), low_row, 1)
                    before = here
                    made = jnp.where(keep_row, moved, jnp.concatenate([moved[15:], moved[:15]]))
                    to_cols = pl.ds(pl.multiple_of(base + j * LANES, LANES), LANES)
                    for t in range(16):
                        out[part, 0, to_rows[t], to_cols] += made[t]


def local(probe_wave, propagator, object_slices, positions, intensities):
    count = lax.axis_size("scan")
    size = probe_wave.shape[1]
    columns = object_slices.shape[3] // LANES
    vmem = pl.BlockSpec(memory_space=pltpu.VMEM)
    smem = pl.BlockSpec(memory_space=pltpu.SMEM)
    anywhere = pl.BlockSpec(memory_space=pl.ANY)
    hbm = pl.BlockSpec(memory_space=pltpu.HBM)
    dma = pltpu.SemaphoreType.DMA
    pos, tiles = pl.pallas_call(
        functools.partial(positions_kernel, count),
        out_shape=[
            jax.ShapeDtypeStruct((8, LANES), jnp.int32),
            jax.ShapeDtypeStruct((2, columns, 16, 8, LANES), F32),
        ],
        in_specs=[hbm, hbm],
        out_specs=[vmem, vmem],
        scratch_shapes=[
            pltpu.SMEM((2, 2), jnp.int32), pltpu.VMEM((8, LANES), jnp.int32), pltpu.VMEM((4, 8, LANES), jnp.int32),
            dma, dma((2, columns)), dma((4,)), dma((4,))],
        compiler_params=pltpu.CompilerParams(
            collective_id=0, has_side_effects=True, vmem_limit_bytes=16 * 2**20),
        name="share_positions",
    )(positions, object_slices.reshape(2, 16, 8, object_slices.shape[3]))

    got = pl.pallas_call(
        functools.partial(chain_kernel, count),
        out_shape=jax.ShapeDtypeStruct((REACH, 2, 2, 128, size), BF16),
        in_specs=[smem, vmem, hbm, hbm, hbm, hbm],
        out_specs=vmem,
        scratch_shapes=[
            pltpu.VMEM((10, 2, 128, size), BF16),
            pltpu.VMEM((4, 2, size, size), BF16),
            pltpu.VMEM((size, size), F32),
            pltpu.VMEM((4, 4, 2, 128, size), BF16),
            pltpu.VMEM((2, 2, 2, 128, size), BF16),
            pltpu.VMEM((2, 2, 128, size), BF16),
            pltpu.VMEM((2, 2, 128, size), BF16),
            pltpu.VMEM((2, size, size), BF16),
            pltpu.VMEM((2, size, size), BF16),
        ]
        + [pltpu.VMEM((2, 2 * size, 2 * size), BF16)] * 2
        + [
            pltpu.VMEM((2 * size, size), BF16),
            pltpu.VMEM((size, 2 * size), BF16),
            pltpu.VMEM((4, 2, size, size), BF16),
            dma((3,)), dma((10,)), dma((4, 4)), dma, dma((2,)), dma((2,)), dma((2,)), dma,
            dma, dma, dma((4, 4)), dma((REACH, 2)), dma, dma((4,)), dma((2,)), dma, dma((2, 2)),
        ],
        compiler_params=pltpu.CompilerParams(
            collective_id=1, has_side_effects=True, vmem_limit_bytes=40 * 2**20),
        name="chain",
    )(pos, tiles, intensities, probe_wave, propagator, dft_table(size))

    return pl.pallas_call(
        add_kernel,
        out_shape=jax.ShapeDtypeStruct(object_slices.shape, F32),
        in_specs=[smem, vmem],
        out_specs=vmem,
        compiler_params=pltpu.CompilerParams(vmem_limit_bytes=24 * 2**20),
        name="add_gradients",
    )(pos, got)


def solution(mesh):
    in_specs = (P(), P(), P(None, "cuts", "scan", None), P("scan", None), P("scan", None, None))
    out_specs = P(None, "cuts", "scan", None)
    return jax.shard_map(local, mesh=mesh, in_specs=in_specs, out_specs=out_specs, check_vma=False)
```

```python
import functools
import math

import jax
import jax.numpy as jnp
import numpy as np
from jax import lax
from jax.experimental import pallas as pl
from jax.experimental.pallas import tpu as pltpu
from jax.sharding import PartitionSpec as P

MESH = pl.DeviceIdType.MESH
BF16 = jnp.bfloat16
F32 = jnp.float32
REACH = 5
LANES = 128


def dft_table(length):
    serial = np.arange(length, dtype=np.int32)
    angle_index = serial[:, None] * serial[None, :] % length
    angle = angle_index.astype(np.float32) * np.float32(2.0 * math.pi / length)
    scale = np.float32(1.0 / math.sqrt(length))
    return jnp.asarray(
        np.stack([np.cos(angle) * scale, -np.sin(angle) * scale]), dtype=BF16
    )


def place():
    me = lax.axis_index("scan")
    cut = lax.axis_index("cuts")
    return me, cut, lax.rem(me, 2)


def wrapped(index, count):
    return lax.rem(index + 2 * count, count)


def worker(me, d, m, count):
    band = wrapped(me - d, count)
    return wrapped(me - d + 2, count), 2 * lax.rem(band, 2) + m


def column_split(column, width, window):
    base = jnp.minimum(column // LANES * LANES, width - window - LANES)
    return pl.multiple_of(base, LANES), column - base


def positions_kernel(count, pos_ref, band, pos_out, tiles, pos_own, tile, pos_in, load_sem, band_sem, psend, precv):
    me, cut, parity = place()
    loads = [pltpu.make_async_copy(pos_ref, pos_own, load_sem)] + [
        pltpu.make_async_copy(
            band.at[part, :, :, pl.ds(n * LANES, LANES)], tiles.at[part, n], band_sem.at[part, n])
        for part in range(2)
        for n in range(tiles.shape[1])
    ]
    for load in loads:
        load.start()
    barrier = pltpu.get_barrier_semaphore()
    for d in range(1, REACH):
        pl.semaphore_signal(barrier, inc=1, device_id=(wrapped(me - d, count), cut), device_id_type=MESH)
    loads[0].wait()
    lane = lax.broadcasted_iota(jnp.int32, (8, LANES), 1)
    values = jnp.zeros((8, LANES), jnp.int32)
    for n in range(4):
        values = jnp.where(lane == n, pos_own[n // 2, n % 2], values)
    tile[...] = values
    pos_out[...] = values
    pl.semaphore_wait(barrier, REACH - 1)
    copies = []
    for d in range(1, REACH):
        copy = pltpu.make_async_remote_copy(
            src_ref=tile, dst_ref=pos_in.at[d - 1], send_sem=psend.at[d - 1], recv_sem=precv.at[d - 1],
            device_id=(wrapped(me + d, count), cut), device_id_type=MESH)
        copy.start()
        copies.append(copy)
    for d in range(1, REACH):
        copies[d - 1].wait()
        pos_out[d:d + 1] = pos_in[d - 1, 0:1]
    for load in loads[1:]:
        load.wait()


def pack(stage, tiles, slot, row, column):
    window, width = stage.shape[3], tiles.shape[1] * LANES
    lane = lax.broadcasted_iota(jnp.int32, (16, 8, LANES), 2)
    sub = lax.broadcasted_iota(jnp.int32, (16, 8, LANES), 1)
    offset = lax.rem(row, 128)
    tile_row, low_row = offset // 8, lax.rem(offset, 8)
    tile_column = jnp.minimum(column // LANES, (width - window) // LANES - 1)
    shift = column - tile_column * LANES
    turn = lax.rem(LANES - shift, LANES)
    lift = lax.rem(8 - low_row, 8)
    keep = lane + shift < LANES
    keep_row = sub + low_row < 8
    rows = [lax.rem(tile_row + t, 16) for t in range(16)]

    def one_part(part, carry):
        turned = []
        for j in range(window // LANES + 1):
            turned.append(pltpu.roll(
                jnp.stack([tiles[part, tile_column + j, rows[t]] for t in range(16)]), turn, 2))
        for j in range(window // LANES):
            lifted = pltpu.roll(jnp.where(keep, turned[j], turned[j + 1]), lift, 1)
            made = jnp.where(keep_row, lifted, jnp.concatenate([lifted[1:], lifted[:1]]))
            stage[slot, part, :, j * LANES:(j + 1) * LANES] = made.reshape(128, LANES).astype(BF16)
        return carry
    lax.fori_loop(0, 2, one_part, 0)


def chain_kernel(count, row_ref, tiles, int_ref, probe_ref, prop_ref, table_ref, got,
                 stage, win, intensity, out, edge, cross, back, prop, table,
                 bigs, bigs_t, upright, flat, waves,
                 load_sem, win_send, win_recv, self_sem, edge_send, edge_recv, cross_send, cross_self,
                 isend, irecv, out_send, out_recv, out_self, back_send, back_recv, back_self, last_send):
    me, cut, parity = place()
    size = flat.shape[0]
    slices = win.shape[0]
    active = (cut // 2) == parity
    half = lax.rem(cut, 2)
    behind, ahead = wrapped(me - 2, count), wrapped(me + 2, count)

    def owner(d, k):
        return wrapped(me - 2 + d, count), jnp.int32(k)

    def is_self(d, m):
        return cut == 2 * parity + m if d == 2 else None

    def either(same, remote, here):
        if same is None:
            remote()
        else:
            pl.when(jnp.logical_not(same))(remote)
            if here is not None:
                pl.when(same)(here)

    loads = [
        pltpu.make_async_copy(src, dst, load_sem.at[n])
        for n, (src, dst) in enumerate(((probe_ref, waves.at[0]), (prop_ref, prop), (table_ref, table)))
    ]
    for load in loads:
        load.start()

    barrier = pltpu.get_barrier_semaphore()

    def greet(device):
        pl.semaphore_signal(barrier, inc=1, device_id=device, device_id_type=MESH)

    greet((behind, cut))
    greet((ahead, cut))
    for m in range(2):
        for d in (1, 2, 3):
            either(is_self(d, m), lambda: greet(worker(me, d, m, count)), None)
        either(is_self(2, m), lambda: greet(worker(me, 2, m, count)), None)

    @pl.when(active)
    def _():
        for k in range(4):
            for d in (1, 2, 3):
                either(cut == k if d == 2 else None, lambda: greet(owner(d, k)), None)
            either(cut == k, lambda: greet(owner(2, k)), None)

    def pack_all(d):
        for m in range(2):
            pack(stage, tiles, d * 2 + m, row_ref[d, 2 * m], row_ref[d, 2 * m + 1])

    pack_all(0)
    pack_all(4)
    pl.semaphore_wait(barrier, jnp.where(active, 22, 10))

    def unit(s, e):
        return win.at[s, :, pl.ds(e * 128, 128), :]

    def window_copy(d, m):
        return pltpu.make_async_remote_copy(
            src_ref=stage.at[d * 2 + m], dst_ref=unit(cut, d),
            send_sem=win_send.at[d * 2 + m], recv_sem=win_recv.at[cut, d],
            device_id=worker(me, d, m, count), device_id_type=MESH)

    def window_here(m):
        return pltpu.make_async_copy(stage.at[4 + m], unit(cut, 2), self_sem)

    def edge_copy(n):
        return pltpu.make_async_remote_copy(
            src_ref=stage.at[pl.ds(8 * n, 2)], dst_ref=edge.at[n],
            send_sem=edge_send.at[n], recv_sem=edge_recv.at[n],
            device_id=((ahead, behind)[n], cut), device_id_type=MESH)

    def cross_copy(m):
        return pltpu.make_async_remote_copy(
            src_ref=cross.at[m], dst_ref=unit(cut, 0), send_sem=cross_send.at[m], recv_sem=win_recv.at[cut, 0],
            device_id=(me, 2 * parity + m), device_id_type=MESH)

    def cross_here(m):
        return pltpu.make_async_copy(cross.at[m], unit(cut, 0), cross_self)

    def window_arrival(s, e):
        return pltpu.make_async_copy(stage.at[0], unit(s, e), win_recv.at[s, e])

    def block_copy(d, k):
        return pltpu.make_async_remote_copy(
            src_ref=out.at[k, d], dst_ref=got.at[d, half],
            send_sem=out_send.at[k, d], recv_sem=out_recv.at[d, half],
            device_id=owner(d, k), device_id_type=MESH)

    def block_here():
        return pltpu.make_async_copy(out.at[cut, 2], got.at[2, half], out_self)

    def back_copy(k):
        return pltpu.make_async_remote_copy(
            src_ref=out.at[k, 0], dst_ref=back.at[half], send_sem=back_send.at[k], recv_sem=back_recv.at[half],
            device_id=(me, jnp.int32(k)), device_id_type=MESH)

    def back_here():
        return pltpu.make_async_copy(out.at[cut, 0], back.at[half], back_self)

    def last_copy(m, n):
        return pltpu.make_async_remote_copy(
            src_ref=back.at[m], dst_ref=got.at[4 * n, m], send_sem=last_send.at[m, n], recv_sem=out_recv.at[4 * n, m],
            device_id=((behind, ahead)[n], cut), device_id_type=MESH)

    icopy = pltpu.make_async_remote_copy(
        src_ref=int_ref.at[half], dst_ref=intensity, send_sem=isend, recv_sem=irecv,
        device_id=(ahead, cut), device_id_type=MESH)

    for n in range(2):
        edge_copy(n).start()
    for d in (1, 3, 2):
        pack_all(d)
        for m in range(2):
            either(is_self(d, m), lambda: window_copy(d, m).start(), lambda: window_here(m).start())

    def dot(a, b):
        return jnp.dot(a, b, preferred_element_type=F32)

    def left(big):
        made = dot(big[...], upright[...])
        flat[:, :size] = made[:size].astype(BF16)
        flat[:, size:] = made[size:].astype(BF16)

    for load in loads:
        load.wait()

    def spread_out(big, re, im):
        big[:size, :size] = re
        big[:size, size:] = -im
        big[size:, :size] = im
        big[size:, size:] = re

    @pl.when(active)
    def _():
        icopy.start()
        upright[:size] = prop[0]
        upright[size:] = prop[1]
        spread_out(bigs.at[0], prop[0], prop[1])
        spread_out(bigs_t.at[0], prop[0].T, -prop[1].T)
        spread_out(bigs_t.at[1], table[0], table[1])
        made = dot(bigs_t[1], upright[...]).astype(BF16)
        spread_out(bigs.at[1], made[:size], made[size:])
        spread_out(bigs_t.at[1], made[:size].T, -made[size:].T)

    for n in range(2):
        edge_copy(n).wait_recv()
    for m in range(2):
        low = lax.broadcasted_iota(jnp.int32, (128, size), 0) < 128 - lax.rem(row_ref[2, 2 * m], 128)
        for part in range(2):
            cross[m, part] = jnp.where(
                low, edge[0, m, part].astype(F32), edge[1, m, part].astype(F32)).astype(BF16)
        either(is_self(2, m), lambda: cross_copy(m).start(), lambda: cross_here(m).start())

    @pl.when(active)
    def _():
        offset = lax.rem(row_ref[2, 2 * half], 128)
        head = lax.broadcasted_iota(jnp.int32, (128, size), 0) < 128 - offset

        def window_rows(s, part, e):
            top = win[s, part, e * 128:(e + 1) * 128, :].astype(F32)
            after = (e + 1) % 4
            low = win[s, part, after * 128:(after + 1) * 128, :].astype(F32)
            return jnp.where(head, top, low)

        def enter(s):
            for e in range(4):
                same, here = None, None
                if e == 0:
                    same, here = cut == s, lambda: cross_here(half).wait()
                elif e == 2:
                    same, here = cut == s, lambda: window_here(half).wait()
                either(same, lambda: window_arrival(s, e).wait(), here)
            for e in range(4):
                rows = slice(e * 128, (e + 1) * 128)
                rows_im = slice(size + e * 128, size + (e + 1) * 128)
                w_re, w_im = window_rows(s, 0, e), window_rows(s, 1, e)
                p_re, p_im = waves[s, 0, rows].astype(F32), waves[s, 1, rows].astype(F32)
                upright[rows] = (p_re * w_re - p_im * w_im).astype(BF16)
                upright[rows_im] = (p_re * w_im + p_im * w_re).astype(BF16)

        def forward(s, carry):
            enter(s)
            left(bigs.at[0])
            made = dot(flat[...], bigs_t[0])
            waves[s + 1, 0] = made[:, :size].astype(BF16)
            waves[s + 1, 1] = made[:, size:].astype(BF16)
            return carry
        lax.fori_loop(0, slices - 1, forward, 0)

        enter(slices - 1)
        left(bigs.at[1])
        icopy.wait()
        made = dot(flat[...], bigs_t[1])
        for e in range(4):
            rows = slice(e * 128, (e + 1) * 128)
            re, im = made[rows, :size], made[rows, size:]
            excess = re * re + im * im - intensity[rows]
            flat[rows, :size] = (excess * re).astype(BF16)
            flat[rows, size:] = (excess * im).astype(BF16)

        def backward(n, carry):
            s = slices - 1 - n
            which = jnp.where(n == 0, 1, 0)
            made = dot(flat[...], bigs[which])
            upright[:size] = made[:, :size].astype(BF16)
            upright[size:] = made[:, size:].astype(BF16)
            made = dot(bigs_t[which], upright[...])
            terms = []
            for e in range(4):
                rows = slice(e * 128, (e + 1) * 128)
                g_re, g_im = made[rows], made[size + e * 128:size + (e + 1) * 128]
                p_re, p_im = waves[s, 0, rows].astype(F32), waves[s, 1, rows].astype(F32)
                terms.append((p_re * g_re + p_im * g_im, p_re * g_im - p_im * g_re))
            for e in range(4):
                for part in range(2):
                    out[s, e, part] = jnp.where(head, terms[e][part], terms[e - 1][part]).astype(BF16)
            either(cut == s, lambda: back_copy(s).start(), lambda: back_here().start())
            for d in (1, 3, 2):
                either(cut == s if d == 2 else None,
                       lambda: block_copy(d, s).start(), lambda: block_here().start())
            for e in range(4):
                rows = slice(e * 128, (e + 1) * 128)
                g_re, g_im = made[rows], made[size + e * 128:size + (e + 1) * 128]
                w_re, w_im = window_rows(s, 0, e), window_rows(s, 1, e)
                flat[rows, :size] = (w_re * g_re + w_im * g_im).astype(BF16)
                flat[rows, size:] = (w_re * g_im - w_im * g_re).astype(BF16)
            return carry
        lax.fori_loop(0, slices, backward, 0)

    for m in range(2):
        either(is_self(2, m),
               lambda: pltpu.make_async_copy(out.at[0, 0], back.at[m], back_recv.at[m]).wait(),
               lambda: back_here().wait())
        for n in range(2):
            last_copy(m, n).start()

    for n in range(2):
        edge_copy(n).wait_send()
    for m in range(2):
        either(is_self(2, m), lambda: cross_copy(m).wait_send(), None)
        for d in (1, 2, 3):
            either(is_self(d, m), lambda: window_copy(d, m).wait_send(), None)

    @pl.when(active)
    def _():
        for k in range(4):
            either(cut == k, lambda: back_copy(k).wait_send(), None)
            for d in (1, 2, 3):
                either(cut == k if d == 2 else None,
                       lambda: block_copy(d, k).wait_send(), lambda: block_here().wait())

    for m in range(2):
        for d in range(REACH):
            either(is_self(d, m),
                   lambda: pltpu.make_async_copy(out.at[0, 0], got.at[d, m], out_recv.at[d, m]).wait(), None)
        for n in range(2):
            last_copy(m, n).wait_send()


def add_kernel(pos_ref, got, out, acc):
    width = out.shape[3]
    window = got.shape[4]
    acc[...] = jnp.zeros_like(acc)
    row = 8 * lax.broadcasted_iota(jnp.int32, (16, 8, LANES), 0) + lax.broadcasted_iota(jnp.int32, (16, 8, LANES), 1)
    lane = lax.broadcasted_iota(jnp.int32, (16, 8, LANES), 2)
    sub = lax.broadcasted_iota(jnp.int32, (17, 8, LANES), 1)
    count = window // LANES
    zero = jnp.zeros((16, 8, LANES), F32)
    gap = jnp.zeros((1, 8, LANES), F32)
    for d in range(REACH):
        for m in range(2):
            offset = lax.rem(pos_ref[d, 2 * m], 128)
            tile_row, low_row = offset // 8, lax.rem(offset, 8)
            base, shift = column_split(pos_ref[d, 2 * m + 1], width, window)
            turn = lax.rem(shift, LANES)
            mine = None
            if d == 0:
                mine = row < 128 - offset
            elif d == REACH - 1:
                mine = row >= 128 - offset
            keep = lane >= shift
            keep_row = sub >= low_row
            to_rows = pl.ds(pl.multiple_of(tile_row * 8, 8), 136)
            for part in range(2):
                before = zero
                for j in range(count + 1):
                    here = zero
                    if j < count:
                        here = got[d, m, part, :, j * LANES:(j + 1) * LANES].astype(F32).reshape(16, 8, LANES)
                        if mine is not None:
                            here = jnp.where(mine, here, 0.0)
                        here = pltpu.roll(here, turn, 2)
                    moved = pltpu.roll(jnp.where(keep, here, before), low_row, 1)
                    before = here
                    made = jnp.where(keep_row, jnp.concatenate([moved, gap]), jnp.concatenate([gap, moved]))
                    to_cols = pl.ds(pl.multiple_of(base + j * LANES, LANES), LANES)
                    acc[part, to_rows, to_cols] += made.reshape(136, LANES)
    out[:, 0] = acc[:, :128] + acc[:, 128:]


def local(probe_wave, propagator, object_slices, positions, intensities):
    count = lax.axis_size("scan")
    size = probe_wave.shape[1]
    columns = object_slices.shape[3] // LANES
    vmem = pl.BlockSpec(memory_space=pltpu.VMEM)

    def kept(x):
        return pltpu.with_memory_space_constraint(x, pltpu.HBM)

    smem = pl.BlockSpec(memory_space=pltpu.SMEM)
    anywhere = pl.BlockSpec(memory_space=pl.ANY)
    hbm = pl.BlockSpec(memory_space=pltpu.HBM)
    dma = pltpu.SemaphoreType.DMA
    pos, tiles = pl.pallas_call(
        functools.partial(positions_kernel, count),
        out_shape=[
            jax.ShapeDtypeStruct((8, LANES), jnp.int32),
            jax.ShapeDtypeStruct((2, columns, 16, 8, LANES), F32),
        ],
        in_specs=[hbm, hbm],
        out_specs=[vmem, vmem],
        scratch_shapes=[
            pltpu.SMEM((2, 2), jnp.int32), pltpu.VMEM((8, LANES), jnp.int32), pltpu.VMEM((4, 8, LANES), jnp.int32),
            dma, dma((2, columns)), dma((4,)), dma((4,))],
        compiler_params=pltpu.CompilerParams(
            collective_id=0, has_side_effects=True, vmem_limit_bytes=16 * 2**20),
        name="share_positions",
    )(kept(positions), kept(object_slices.reshape(2, 16, 8, object_slices.shape[3])))

    got = pl.pallas_call(
        functools.partial(chain_kernel, count),
        out_shape=jax.ShapeDtypeStruct((REACH, 2, 2, 128, size), BF16),
        in_specs=[smem, vmem, hbm, hbm, hbm, hbm],
        out_specs=vmem,
        scratch_shapes=[
            pltpu.VMEM((10, 2, 128, size), BF16),
            pltpu.VMEM((4, 2, size, size), BF16),
            pltpu.VMEM((size, size), F32),
            pltpu.VMEM((4, 4, 2, 128, size), BF16),
            pltpu.VMEM((2, 2, 2, 128, size), BF16),
            pltpu.VMEM((2, 2, 128, size), BF16),
            pltpu.VMEM((2, 2, 128, size), BF16),
            pltpu.VMEM((2, size, size), BF16),
            pltpu.VMEM((2, size, size), BF16),
        ]
        + [pltpu.VMEM((2, 2 * size, 2 * size), BF16)] * 2
        + [
            pltpu.VMEM((2 * size, size), BF16),
            pltpu.VMEM((size, 2 * size), BF16),
            pltpu.VMEM((4, 2, size, size), BF16),
            dma((3,)), dma((10,)), dma((4, 4)), dma, dma((2,)), dma((2,)), dma((2,)), dma,
            dma, dma, dma((4, 4)), dma((REACH, 2)), dma, dma((4,)), dma((2,)), dma, dma((2, 2)),
        ],
        compiler_params=pltpu.CompilerParams(
            collective_id=1, has_side_effects=True, vmem_limit_bytes=40 * 2**20),
        name="chain",
    )(pos, tiles, kept(intensities), kept(probe_wave), kept(propagator), kept(dft_table(size)))

    return pl.pallas_call(
        add_kernel,
        out_shape=jax.ShapeDtypeStruct(object_slices.shape, F32),
        in_specs=[smem, vmem],
        out_specs=vmem,
        scratch_shapes=[pltpu.VMEM((2, 256, object_slices.shape[3]), F32)],
        compiler_params=pltpu.CompilerParams(vmem_limit_bytes=24 * 2**20),
        name="add_gradients",
    )(pos, got)


def solution(mesh):
    in_specs = (P(), P(), P(None, "cuts", "scan", None), P("scan", None), P("scan", None, None))
    out_specs = P(None, "cuts", "scan", None)
    return jax.shard_map(local, mesh=mesh, in_specs=in_specs, out_specs=out_specs, check_vma=False)
```

```python
import functools
import math

import jax
import jax.numpy as jnp
import numpy as np
from jax import lax
from jax.experimental import pallas as pl
from jax.experimental.pallas import tpu as pltpu
from jax.sharding import PartitionSpec as P

MESH = pl.DeviceIdType.MESH
BF16 = jnp.bfloat16
F32 = jnp.float32
REACH = 5
LANES = 128


def dft_table(length):
    serial = np.arange(length, dtype=np.int32)
    angle_index = serial[:, None] * serial[None, :] % length
    angle = angle_index.astype(np.float32) * np.float32(2.0 * math.pi / length)
    scale = np.float32(1.0 / math.sqrt(length))
    return jnp.asarray(
        np.stack([np.cos(angle) * scale, -np.sin(angle) * scale]), dtype=BF16
    )


def place():
    me = lax.axis_index("scan")
    cut = lax.axis_index("cuts")
    return me, cut, lax.rem(me, 2)


def wrapped(index, count):
    return lax.rem(index + 2 * count, count)


def worker(me, d, m, count):
    band = wrapped(me - d, count)
    return wrapped(me - d + 2, count), 2 * lax.rem(band, 2) + m


def column_split(column, width, window):
    base = jnp.minimum(column // LANES * LANES, width - window - LANES)
    return pl.multiple_of(base, LANES), column - base


def positions_kernel(count, pos_ref, band, pos_out, tiles, pos_own, tile, pos_in, load_sem, band_sem, psend, precv):
    me, cut, parity = place()
    barrier = pltpu.get_barrier_semaphore()
    for d in range(1, REACH):
        pl.semaphore_signal(barrier, inc=1, device_id=(wrapped(me - d, count), cut), device_id_type=MESH)
    own_load = pltpu.make_async_copy(pos_ref, pos_own, load_sem)
    own_load.start()
    loads = [
        pltpu.make_async_copy(
            band.at[part, :, :, pl.ds(n * LANES, LANES)], tiles.at[part, n], band_sem.at[part, n])
        for part in range(2)
        for n in range(tiles.shape[1])
    ]
    own_load.wait()
    lane = lax.broadcasted_iota(jnp.int32, (8, LANES), 1)
    values = jnp.zeros((8, LANES), jnp.int32)
    for n in range(4):
        values = jnp.where(lane == n, pos_own[n // 2, n % 2], values)
    tile[...] = values
    pos_out[...] = values
    pl.semaphore_wait(barrier, REACH - 1)
    copies = []
    for d in range(1, REACH):
        copy = pltpu.make_async_remote_copy(
            src_ref=tile, dst_ref=pos_in.at[d - 1], send_sem=psend.at[d - 1], recv_sem=precv.at[d - 1],
            device_id=(wrapped(me + d, count), cut), device_id_type=MESH)
        copy.start()
        copies.append(copy)
    for load in loads:
        load.start()
    for d in range(1, REACH):
        copies[d - 1].wait()
        pos_out[d:d + 1] = pos_in[d - 1, 0:1]
    for load in loads:
        load.wait()


def pack(stage, tiles, slot, row, column):
    window, width = stage.shape[3], tiles.shape[1] * LANES
    lane = lax.broadcasted_iota(jnp.int32, (16, 8, LANES), 2)
    sub = lax.broadcasted_iota(jnp.int32, (16, 8, LANES), 1)
    offset = lax.rem(row, 128)
    tile_row, low_row = offset // 8, lax.rem(offset, 8)
    tile_column = jnp.minimum(column // LANES, (width - window) // LANES - 1)
    shift = column - tile_column * LANES
    turn = lax.rem(LANES - shift, LANES)
    lift = lax.rem(8 - low_row, 8)
    keep = lane + shift < LANES
    keep_row = sub + low_row < 8
    rows = [lax.rem(tile_row + t, 16) for t in range(16)]

    def one_part(part, carry):
        turned = []
        for j in range(window // LANES + 1):
            turned.append(pltpu.roll(
                jnp.stack([tiles[part, tile_column + j, rows[t]] for t in range(16)]), turn, 2))
        for j in range(window // LANES):
            lifted = pltpu.roll(jnp.where(keep, turned[j], turned[j + 1]), lift, 1)
            made = jnp.where(keep_row, lifted, jnp.concatenate([lifted[1:], lifted[:1]]))
            stage[slot, part, :, j * LANES:(j + 1) * LANES] = made.reshape(128, LANES).astype(BF16)
        return carry
    lax.fori_loop(0, 2, one_part, 0)


def chain_kernel(count, row_ref, tiles, int_ref, probe_ref, prop_ref, table_ref, got,
                 stage, win, intensity, out, edge, cross, back, prop, table,
                 bigs, bigs_t, upright, flat, waves,
                 load_sem, win_send, win_recv, self_sem, edge_send, edge_recv, cross_send, cross_self,
                 isend, irecv, out_send, out_recv, out_self, back_send, back_recv, back_self, last_send):
    me, cut, parity = place()
    size = flat.shape[0]
    slices = win.shape[0]
    active = (cut // 2) == parity
    half = lax.rem(cut, 2)
    behind, ahead = wrapped(me - 2, count), wrapped(me + 2, count)

    def owner(d, k):
        return wrapped(me - 2 + d, count), jnp.int32(k)

    def is_self(d, m):
        return cut == 2 * parity + m if d == 2 else None

    def either(same, remote, here):
        if same is None:
            remote()
        else:
            pl.when(jnp.logical_not(same))(remote)
            if here is not None:
                pl.when(same)(here)

    loads = [
        pltpu.make_async_copy(src, dst, load_sem.at[n])
        for n, (src, dst) in enumerate(((probe_ref, waves.at[0]), (prop_ref, prop), (table_ref, table)))
    ]
    for load in loads:
        load.start()

    barrier = pltpu.get_barrier_semaphore()

    def greet(device):
        pl.semaphore_signal(barrier, inc=1, device_id=device, device_id_type=MESH)

    greet((behind, cut))
    greet((ahead, cut))
    for m in range(2):
        for d in (1, 2, 3):
            either(is_self(d, m), lambda: greet(worker(me, d, m, count)), None)
        either(is_self(2, m), lambda: greet(worker(me, 2, m, count)), None)

    @pl.when(active)
    def _():
        for k in range(4):
            for d in (1, 2, 3):
                either(cut == k if d == 2 else None, lambda: greet(owner(d, k)), None)
            either(cut == k, lambda: greet(owner(2, k)), None)

    def pack_all(d):
        for m in range(2):
            pack(stage, tiles, d * 2 + m, row_ref[d, 2 * m], row_ref[d, 2 * m + 1])

    for d in (0, 4, 1, 3, 2):
        pack_all(d)
    pl.semaphore_wait(barrier, jnp.where(active, 22, 10))

    def unit(s, e):
        return win.at[s, :, pl.ds(e * 128, 128), :]

    def window_copy(d, m):
        return pltpu.make_async_remote_copy(
            src_ref=stage.at[d * 2 + m], dst_ref=unit(cut, d),
            send_sem=win_send.at[d * 2 + m], recv_sem=win_recv.at[cut, d],
            device_id=worker(me, d, m, count), device_id_type=MESH)

    def window_here(m):
        return pltpu.make_async_copy(stage.at[4 + m], unit(cut, 2), self_sem)

    def edge_copy(n):
        return pltpu.make_async_remote_copy(
            src_ref=stage.at[pl.ds(8 * n, 2)], dst_ref=edge.at[n],
            send_sem=edge_send.at[n], recv_sem=edge_recv.at[n],
            device_id=((ahead, behind)[n], cut), device_id_type=MESH)

    def cross_copy(m):
        return pltpu.make_async_remote_copy(
            src_ref=cross.at[m], dst_ref=unit(cut, 0), send_sem=cross_send.at[m], recv_sem=win_recv.at[cut, 0],
            device_id=(me, 2 * parity + m), device_id_type=MESH)

    def cross_here(m):
        return pltpu.make_async_copy(cross.at[m], unit(cut, 0), cross_self)

    def window_arrival(s, e):
        return pltpu.make_async_copy(stage.at[0], unit(s, e), win_recv.at[s, e])

    def block_copy(d, k):
        return pltpu.make_async_remote_copy(
            src_ref=out.at[k, d], dst_ref=got.at[d, half],
            send_sem=out_send.at[k, d], recv_sem=out_recv.at[d, half],
            device_id=owner(d, k), device_id_type=MESH)

    def block_here():
        return pltpu.make_async_copy(out.at[cut, 2], got.at[2, half], out_self)

    def back_copy(k):
        return pltpu.make_async_remote_copy(
            src_ref=out.at[k, 0], dst_ref=back.at[half], send_sem=back_send.at[k], recv_sem=back_recv.at[half],
            device_id=(me, jnp.int32(k)), device_id_type=MESH)

    def back_here():
        return pltpu.make_async_copy(out.at[cut, 0], back.at[half], back_self)

    def last_copy(m, n):
        return pltpu.make_async_remote_copy(
            src_ref=back.at[m], dst_ref=got.at[4 * n, m], send_sem=last_send.at[m, n], recv_sem=out_recv.at[4 * n, m],
            device_id=((behind, ahead)[n], cut), device_id_type=MESH)

    icopy = pltpu.make_async_remote_copy(
        src_ref=int_ref.at[half], dst_ref=intensity, send_sem=isend, recv_sem=irecv,
        device_id=(ahead, cut), device_id_type=MESH)

    for n in range(2):
        edge_copy(n).start()
    for d in (1, 3, 2):
        for m in range(2):
            either(is_self(d, m), lambda: window_copy(d, m).start(), lambda: window_here(m).start())

    def dot(a, b):
        return jnp.dot(a, b, preferred_element_type=F32)

    def left(big):
        made = dot(big[...], upright[...])
        flat[:, :size] = made[:size].astype(BF16)
        flat[:, size:] = made[size:].astype(BF16)

    for load in loads:
        load.wait()

    def spread_out(big, re, im):
        big[:size, :size] = re
        big[:size, size:] = -im
        big[size:, :size] = im
        big[size:, size:] = re

    @pl.when(active)
    def _():
        icopy.start()
        upright[:size] = prop[0]
        upright[size:] = prop[1]
        spread_out(bigs.at[0], prop[0], prop[1])
        spread_out(bigs_t.at[0], prop[0].T, -prop[1].T)
        spread_out(bigs_t.at[1], table[0], table[1])
        made = dot(bigs_t[1], upright[...]).astype(BF16)
        spread_out(bigs.at[1], made[:size], made[size:])
        spread_out(bigs_t.at[1], made[:size].T, -made[size:].T)

    for n in range(2):
        edge_copy(n).wait_recv()
    for m in range(2):
        low = lax.broadcasted_iota(jnp.int32, (128, size), 0) < 128 - lax.rem(row_ref[2, 2 * m], 128)
        for part in range(2):
            cross[m, part] = jnp.where(
                low, edge[0, m, part].astype(F32), edge[1, m, part].astype(F32)).astype(BF16)
        either(is_self(2, m), lambda: cross_copy(m).start(), lambda: cross_here(m).start())

    @pl.when(active)
    def _():
        offset = lax.rem(row_ref[2, 2 * half], 128)
        head = lax.broadcasted_iota(jnp.int32, (128, size), 0) < 128 - offset

        def window_rows(s, part, e):
            top = win[s, part, e * 128:(e + 1) * 128, :].astype(F32)
            after = (e + 1) % 4
            low = win[s, part, after * 128:(after + 1) * 128, :].astype(F32)
            return jnp.where(head, top, low)

        def enter(s):
            for e in range(4):
                same, here = None, None
                if e == 0:
                    same, here = cut == s, lambda: cross_here(half).wait()
                elif e == 2:
                    same, here = cut == s, lambda: window_here(half).wait()
                either(same, lambda: window_arrival(s, e).wait(), here)
            for e in range(4):
                rows = slice(e * 128, (e + 1) * 128)
                rows_im = slice(size + e * 128, size + (e + 1) * 128)
                w_re, w_im = window_rows(s, 0, e), window_rows(s, 1, e)
                p_re, p_im = waves[s, 0, rows].astype(F32), waves[s, 1, rows].astype(F32)
                upright[rows] = (p_re * w_re - p_im * w_im).astype(BF16)
                upright[rows_im] = (p_re * w_im + p_im * w_re).astype(BF16)

        def forward(s, carry):
            enter(s)
            left(bigs.at[0])
            made = dot(flat[...], bigs_t[0])
            waves[s + 1, 0] = made[:, :size].astype(BF16)
            waves[s + 1, 1] = made[:, size:].astype(BF16)
            return carry
        lax.fori_loop(0, slices - 1, forward, 0)

        enter(slices - 1)
        left(bigs.at[1])
        icopy.wait()
        made = dot(flat[...], bigs_t[1])
        for e in range(4):
            rows = slice(e * 128, (e + 1) * 128)
            re, im = made[rows, :size], made[rows, size:]
            excess = re * re + im * im - intensity[rows]
            flat[rows, :size] = (excess * re).astype(BF16)
            flat[rows, size:] = (excess * im).astype(BF16)

        def backward(n, carry):
            s = slices - 1 - n
            which = jnp.where(n == 0, 1, 0)
            made = dot(flat[...], bigs[which])
            upright[:size] = made[:, :size].astype(BF16)
            upright[size:] = made[:, size:].astype(BF16)
            made = dot(bigs_t[which], upright[...])
            terms = []
            for e in range(4):
                rows = slice(e * 128, (e + 1) * 128)
                g_re, g_im = made[rows], made[size + e * 128:size + (e + 1) * 128]
                p_re, p_im = waves[s, 0, rows].astype(F32), waves[s, 1, rows].astype(F32)
                terms.append((p_re * g_re + p_im * g_im, p_re * g_im - p_im * g_re))
            for e in range(4):
                for part in range(2):
                    out[s, e, part] = jnp.where(head, terms[e][part], terms[e - 1][part]).astype(BF16)
            either(cut == s, lambda: back_copy(s).start(), lambda: back_here().start())
            for d in (1, 3, 2):
                either(cut == s if d == 2 else None,
                       lambda: block_copy(d, s).start(), lambda: block_here().start())
            for e in range(4):
                rows = slice(e * 128, (e + 1) * 128)
                g_re, g_im = made[rows], made[size + e * 128:size + (e + 1) * 128]
                w_re, w_im = window_rows(s, 0, e), window_rows(s, 1, e)
                flat[rows, :size] = (w_re * g_re + w_im * g_im).astype(BF16)
                flat[rows, size:] = (w_re * g_im - w_im * g_re).astype(BF16)
            return carry
        lax.fori_loop(0, slices, backward, 0)

    for m in range(2):
        either(is_self(2, m),
               lambda: pltpu.make_async_copy(out.at[0, 0], back.at[m], back_recv.at[m]).wait(),
               lambda: back_here().wait())
        for n in range(2):
            last_copy(m, n).start()

    for n in range(2):
        edge_copy(n).wait_send()
    for m in range(2):
        either(is_self(2, m), lambda: cross_copy(m).wait_send(), None)
        for d in (1, 2, 3):
            either(is_self(d, m), lambda: window_copy(d, m).wait_send(), None)

    @pl.when(active)
    def _():
        for k in range(4):
            either(cut == k, lambda: back_copy(k).wait_send(), None)
            for d in (1, 2, 3):
                either(cut == k if d == 2 else None,
                       lambda: block_copy(d, k).wait_send(), lambda: block_here().wait())

    for m in range(2):
        for d in range(REACH):
            either(is_self(d, m),
                   lambda: pltpu.make_async_copy(out.at[0, 0], got.at[d, m], out_recv.at[d, m]).wait(), None)
        for n in range(2):
            last_copy(m, n).wait_send()


def add_kernel(pos_ref, got, out, acc):
    width = out.shape[3]
    window = got.shape[4]
    acc[...] = jnp.zeros_like(acc)
    row = 8 * lax.broadcasted_iota(jnp.int32, (16, 8, LANES), 0) + lax.broadcasted_iota(jnp.int32, (16, 8, LANES), 1)
    lane = lax.broadcasted_iota(jnp.int32, (16, 8, LANES), 2)
    sub = lax.broadcasted_iota(jnp.int32, (17, 8, LANES), 1)
    count = window // LANES
    zero = jnp.zeros((16, 8, LANES), F32)
    gap = jnp.zeros((1, 8, LANES), F32)
    for d in range(REACH):
        for m in range(2):
            offset = lax.rem(pos_ref[d, 2 * m], 128)
            tile_row, low_row = offset // 8, lax.rem(offset, 8)
            base, shift = column_split(pos_ref[d, 2 * m + 1], width, window)
            turn = lax.rem(shift, LANES)
            mine = None
            if d == 0:
                mine = row < 128 - offset
            elif d == REACH - 1:
                mine = row >= 128 - offset
            keep = lane >= shift
            keep_row = sub >= low_row
            to_rows = pl.ds(pl.multiple_of(tile_row * 8, 8), 136)
            for part in range(2):
                before = zero
                for j in range(count + 1):
                    here = zero
                    if j < count:
                        here = got[d, m, part, :, j * LANES:(j + 1) * LANES].astype(F32).reshape(16, 8, LANES)
                        if mine is not None:
                            here = jnp.where(mine, here, 0.0)
                        here = pltpu.roll(here, turn, 2)
                    moved = pltpu.roll(jnp.where(keep, here, before), low_row, 1)
                    before = here
                    made = jnp.where(keep_row, jnp.concatenate([moved, gap]), jnp.concatenate([gap, moved]))
                    to_cols = pl.ds(pl.multiple_of(base + j * LANES, LANES), LANES)
                    acc[part, to_rows, to_cols] += made.reshape(136, LANES)
    out[:, 0] = acc[:, :128] + acc[:, 128:]


def local(probe_wave, propagator, object_slices, positions, intensities):
    count = lax.axis_size("scan")
    size = probe_wave.shape[1]
    columns = object_slices.shape[3] // LANES
    vmem = pl.BlockSpec(memory_space=pltpu.VMEM)

    def kept(x):
        return pltpu.with_memory_space_constraint(x, pltpu.HBM)

    smem = pl.BlockSpec(memory_space=pltpu.SMEM)
    anywhere = pl.BlockSpec(memory_space=pl.ANY)
    hbm = pl.BlockSpec(memory_space=pltpu.HBM)
    dma = pltpu.SemaphoreType.DMA
    pos, tiles = pl.pallas_call(
        functools.partial(positions_kernel, count),
        out_shape=[
            jax.ShapeDtypeStruct((8, LANES), jnp.int32),
            jax.ShapeDtypeStruct((2, columns, 16, 8, LANES), F32),
        ],
        in_specs=[hbm, hbm],
        out_specs=[vmem, vmem],
        scratch_shapes=[
            pltpu.SMEM((2, 2), jnp.int32), pltpu.VMEM((8, LANES), jnp.int32), pltpu.VMEM((4, 8, LANES), jnp.int32),
            dma, dma((2, columns)), dma((4,)), dma((4,))],
        compiler_params=pltpu.CompilerParams(
            collective_id=0, has_side_effects=True, vmem_limit_bytes=16 * 2**20),
        name="share_positions",
    )(kept(positions), kept(object_slices.reshape(2, 16, 8, object_slices.shape[3])))

    got = pl.pallas_call(
        functools.partial(chain_kernel, count),
        out_shape=jax.ShapeDtypeStruct((REACH, 2, 2, 128, size), BF16),
        in_specs=[smem, vmem, hbm, hbm, hbm, hbm],
        out_specs=vmem,
        scratch_shapes=[
            pltpu.VMEM((10, 2, 128, size), BF16),
            pltpu.VMEM((4, 2, size, size), BF16),
            pltpu.VMEM((size, size), F32),
            pltpu.VMEM((4, 4, 2, 128, size), BF16),
            pltpu.VMEM((2, 2, 2, 128, size), BF16),
            pltpu.VMEM((2, 2, 128, size), BF16),
            pltpu.VMEM((2, 2, 128, size), BF16),
            pltpu.VMEM((2, size, size), BF16),
            pltpu.VMEM((2, size, size), BF16),
        ]
        + [pltpu.VMEM((2, 2 * size, 2 * size), BF16)] * 2
        + [
            pltpu.VMEM((2 * size, size), BF16),
            pltpu.VMEM((size, 2 * size), BF16),
            pltpu.VMEM((4, 2, size, size), BF16),
            dma((3,)), dma((10,)), dma((4, 4)), dma, dma((2,)), dma((2,)), dma((2,)), dma,
            dma, dma, dma((4, 4)), dma((REACH, 2)), dma, dma((4,)), dma((2,)), dma, dma((2, 2)),
        ],
        compiler_params=pltpu.CompilerParams(
            collective_id=1, has_side_effects=True, vmem_limit_bytes=40 * 2**20),
        name="chain",
    )(pos, tiles, kept(intensities), kept(probe_wave), kept(propagator), kept(dft_table(size)))

    return pl.pallas_call(
        add_kernel,
        out_shape=jax.ShapeDtypeStruct(object_slices.shape, F32),
        in_specs=[smem, vmem],
        out_specs=vmem,
        scratch_shapes=[pltpu.VMEM((2, 256, object_slices.shape[3]), F32)],
        compiler_params=pltpu.CompilerParams(vmem_limit_bytes=24 * 2**20),
        name="add_gradients",
    )(pos, got)


def solution(mesh):
    in_specs = (P(), P(), P(None, "cuts", "scan", None), P("scan", None), P("scan", None, None))
    out_specs = P(None, "cuts", "scan", None)
    return jax.shard_map(local, mesh=mesh, in_specs=in_specs, out_specs=out_specs, check_vma=False)
```

```python
import functools
import math

import jax
import jax.numpy as jnp
import numpy as np
from jax import lax
from jax.experimental import pallas as pl
from jax.experimental.pallas import tpu as pltpu
from jax.sharding import PartitionSpec as P

MESH = pl.DeviceIdType.MESH
BF16 = jnp.bfloat16
F32 = jnp.float32
REACH = 5
LANES = 128


def dft_table(length):
    serial = np.arange(length, dtype=np.int32)
    angle_index = serial[:, None] * serial[None, :] % length
    angle = angle_index.astype(np.float32) * np.float32(2.0 * math.pi / length)
    scale = np.float32(1.0 / math.sqrt(length))
    return jnp.asarray(
        np.stack([np.cos(angle) * scale, -np.sin(angle) * scale]), dtype=BF16
    )


def place():
    me = lax.axis_index("scan")
    cut = lax.axis_index("cuts")
    return me, cut, lax.rem(me, 2)


def wrapped(index, count):
    return lax.rem(index + 2 * count, count)


def worker(me, d, m, count):
    band = wrapped(me - d, count)
    return wrapped(me - d + 2, count), 2 * lax.rem(band, 2) + m


def column_split(column, width, window):
    base = jnp.minimum(column // LANES * LANES, width - window - LANES)
    return pl.multiple_of(base, LANES), column - base


def positions_kernel(count, pos_ref, band, pos_out, tiles, pos_own, tile, pos_in, load_sem, band_sem, psend, precv):
    me, cut, parity = place()
    barrier = pltpu.get_barrier_semaphore()
    for d in range(1, REACH):
        pl.semaphore_signal(barrier, inc=1, device_id=(wrapped(me - d, count), cut), device_id_type=MESH)
    own_load = pltpu.make_async_copy(pos_ref, pos_own, load_sem)
    own_load.start()
    loads = [
        pltpu.make_async_copy(
            band.at[part, :, :, pl.ds(n * LANES, LANES)], tiles.at[part, n], band_sem.at[part, n])
        for part in range(2)
        for n in range(tiles.shape[1])
    ]
    own_load.wait()
    lane = lax.broadcasted_iota(jnp.int32, (8, LANES), 1)
    values = jnp.zeros((8, LANES), jnp.int32)
    for n in range(4):
        values = jnp.where(lane == n, pos_own[n // 2, n % 2], values)
    tile[...] = values
    pos_out[...] = values
    pl.semaphore_wait(barrier, REACH - 1)
    copies = []
    for d in range(1, REACH):
        copy = pltpu.make_async_remote_copy(
            src_ref=tile, dst_ref=pos_in.at[d - 1], send_sem=psend.at[d - 1], recv_sem=precv.at[d - 1],
            device_id=(wrapped(me + d, count), cut), device_id_type=MESH)
        copy.start()
        copies.append(copy)
    for load in loads:
        load.start()
    for d in range(1, REACH):
        copies[d - 1].wait()
        pos_out[d:d + 1] = pos_in[d - 1, 0:1]
    for load in loads:
        load.wait()


def pack(stage, tiles, slot, row, column):
    window, width = stage.shape[3], tiles.shape[1] * LANES
    lane = lax.broadcasted_iota(jnp.int32, (16, 8, LANES), 2)
    sub = lax.broadcasted_iota(jnp.int32, (16, 8, LANES), 1)
    offset = lax.rem(row, 128)
    tile_row, low_row = offset // 8, lax.rem(offset, 8)
    tile_column = jnp.minimum(column // LANES, (width - window) // LANES - 1)
    shift = column - tile_column * LANES
    turn = lax.rem(LANES - shift, LANES)
    lift = lax.rem(8 - low_row, 8)
    keep = lane + shift < LANES
    keep_row = sub + low_row < 8
    rows = [lax.rem(tile_row + t, 16) for t in range(16)]

    def one_part(part, carry):
        turned = []
        for j in range(window // LANES + 1):
            turned.append(pltpu.roll(
                jnp.stack([tiles[part, tile_column + j, rows[t]] for t in range(16)]), turn, 2))
        for j in range(window // LANES):
            lifted = pltpu.roll(jnp.where(keep, turned[j], turned[j + 1]), lift, 1)
            made = jnp.where(keep_row, lifted, jnp.concatenate([lifted[1:], lifted[:1]]))
            stage[slot, part, :, j * LANES:(j + 1) * LANES] = made.reshape(128, LANES).astype(BF16)
        return carry
    lax.fori_loop(0, 2, one_part, 0)


def chain_kernel(count, row_ref, tiles, int_ref, probe_ref, prop_ref, table_ref, got,
                 stage, win, intensity, out, edge, cross, back, prop, table,
                 bigs, bigs_t, upright, flat, waves,
                 load_sem, win_send, win_recv, self_sem, edge_send, edge_recv, cross_send, cross_self,
                 isend, irecv, out_send, out_recv, out_self, back_send, back_recv, back_self, last_send):
    me, cut, parity = place()
    size = flat.shape[0]
    slices = win.shape[0]
    active = (cut // 2) == parity
    half = lax.rem(cut, 2)
    behind, ahead = wrapped(me - 2, count), wrapped(me + 2, count)

    def owner(d, k):
        return wrapped(me - 2 + d, count), jnp.int32(k)

    def is_self(d, m):
        return cut == 2 * parity + m if d == 2 else None

    def either(same, remote, here):
        if same is None:
            remote()
        else:
            pl.when(jnp.logical_not(same))(remote)
            if here is not None:
                pl.when(same)(here)

    loads = [
        pltpu.make_async_copy(src, dst, load_sem.at[n])
        for n, (src, dst) in enumerate(((probe_ref, waves.at[0]), (prop_ref, prop), (table_ref, table)))
    ]
    for load in loads:
        load.start()

    barrier = pltpu.get_barrier_semaphore()

    def greet(device):
        pl.semaphore_signal(barrier, inc=1, device_id=device, device_id_type=MESH)

    greet((behind, cut))
    greet((ahead, cut))
    for m in range(2):
        for d in (1, 2, 3):
            either(is_self(d, m), lambda: greet(worker(me, d, m, count)), None)
        either(is_self(2, m), lambda: greet(worker(me, 2, m, count)), None)

    @pl.when(active)
    def _():
        for k in range(4):
            for d in (1, 2, 3):
                either(cut == k if d == 2 else None, lambda: greet(owner(d, k)), None)
            either(cut == k, lambda: greet(owner(2, k)), None)

    def pack_all(d):
        for m in range(2):
            pack(stage, tiles, d * 2 + m, row_ref[d, 2 * m], row_ref[d, 2 * m + 1])

    for d in (0, 4, 1, 3, 2):
        pack_all(d)
    pl.semaphore_wait(barrier, jnp.where(active, 22, 10))

    def unit(s, e):
        return win.at[s, :, pl.ds(e * 128, 128), :]

    def window_copy(d, m):
        return pltpu.make_async_remote_copy(
            src_ref=stage.at[d * 2 + m], dst_ref=unit(cut, d),
            send_sem=win_send.at[d * 2 + m], recv_sem=win_recv.at[cut, d],
            device_id=worker(me, d, m, count), device_id_type=MESH)

    def window_here(m):
        return pltpu.make_async_copy(stage.at[4 + m], unit(cut, 2), self_sem)

    def edge_copy(n):
        return pltpu.make_async_remote_copy(
            src_ref=stage.at[pl.ds(8 * n, 2)], dst_ref=edge.at[n],
            send_sem=edge_send.at[n], recv_sem=edge_recv.at[n],
            device_id=((ahead, behind)[n], cut), device_id_type=MESH)

    def cross_copy(m):
        return pltpu.make_async_remote_copy(
            src_ref=cross.at[m], dst_ref=unit(cut, 0), send_sem=cross_send.at[m], recv_sem=win_recv.at[cut, 0],
            device_id=(me, 2 * parity + m), device_id_type=MESH)

    def cross_here(m):
        return pltpu.make_async_copy(cross.at[m], unit(cut, 0), cross_self)

    def window_arrival(s, e):
        return pltpu.make_async_copy(stage.at[0], unit(s, e), win_recv.at[s, e])

    def block_copy(d, k):
        return pltpu.make_async_remote_copy(
            src_ref=out.at[k, d], dst_ref=got.at[d, half],
            send_sem=out_send.at[k, d], recv_sem=out_recv.at[d, half],
            device_id=owner(d, k), device_id_type=MESH)

    def block_here():
        return pltpu.make_async_copy(out.at[cut, 2], got.at[2, half], out_self)

    def back_copy(k):
        return pltpu.make_async_remote_copy(
            src_ref=out.at[k, 0], dst_ref=back.at[half], send_sem=back_send.at[k], recv_sem=back_recv.at[half],
            device_id=(me, jnp.int32(k)), device_id_type=MESH)

    def back_here():
        return pltpu.make_async_copy(out.at[cut, 0], back.at[half], back_self)

    def last_copy(m, n):
        return pltpu.make_async_remote_copy(
            src_ref=back.at[m], dst_ref=got.at[4 * n, m], send_sem=last_send.at[m, n], recv_sem=out_recv.at[4 * n, m],
            device_id=((behind, ahead)[n], cut), device_id_type=MESH)

    icopy = pltpu.make_async_remote_copy(
        src_ref=int_ref.at[half], dst_ref=intensity, send_sem=isend, recv_sem=irecv,
        device_id=(ahead, cut), device_id_type=MESH)

    for n in range(2):
        edge_copy(n).start()
    for d in (1, 3, 2):
        for m in range(2):
            either(is_self(d, m), lambda: window_copy(d, m).start(), lambda: window_here(m).start())

    def dot(a, b):
        return jnp.dot(a, b, preferred_element_type=F32)

    def left(big):
        made = dot(big[...], upright[...])
        flat[:, :size] = made[:size].astype(BF16)
        flat[:, size:] = made[size:].astype(BF16)

    for load in loads:
        load.wait()

    def spread_out(big, re, im):
        big[:size, :size] = re
        big[:size, size:] = -im
        big[size:, :size] = im
        big[size:, size:] = re

    @pl.when(active)
    def _():
        icopy.start()
        upright[:size] = prop[0]
        upright[size:] = prop[1]
        spread_out(bigs.at[0], prop[0], prop[1])
        spread_out(bigs_t.at[0], prop[0].T, -prop[1].T)
        spread_out(bigs_t.at[1], table[0], table[1])
        made = dot(bigs_t[1], upright[...]).astype(BF16)
        spread_out(bigs.at[1], made[:size], made[size:])
        spread_out(bigs_t.at[1], made[:size].T, -made[size:].T)

    for n in range(2):
        edge_copy(n).wait_recv()
    for m in range(2):
        low = lax.broadcasted_iota(jnp.int32, (128, size), 0) < 128 - lax.rem(row_ref[2, 2 * m], 128)
        for part in range(2):
            cross[m, part] = jnp.where(
                low, edge[0, m, part].astype(F32), edge[1, m, part].astype(F32)).astype(BF16)
        either(is_self(2, m), lambda: cross_copy(m).start(), lambda: cross_here(m).start())

    @pl.when(active)
    def _():
        offset = lax.rem(row_ref[2, 2 * half], 128)
        head = lax.broadcasted_iota(jnp.int32, (128, size), 0) < 128 - offset

        def window_rows(s, part, e):
            top = win[s, part, e * 128:(e + 1) * 128, :].astype(F32)
            after = (e + 1) % 4
            low = win[s, part, after * 128:(after + 1) * 128, :].astype(F32)
            return jnp.where(head, top, low)

        def enter(s):
            for e in range(4):
                same, here = None, None
                if e == 0:
                    same, here = cut == s, lambda: cross_here(half).wait()
                elif e == 2:
                    same, here = cut == s, lambda: window_here(half).wait()
                either(same, lambda: window_arrival(s, e).wait(), here)
            for e in range(4):
                rows = slice(e * 128, (e + 1) * 128)
                rows_im = slice(size + e * 128, size + (e + 1) * 128)
                w_re, w_im = window_rows(s, 0, e), window_rows(s, 1, e)
                p_re, p_im = waves[s, 0, rows].astype(F32), waves[s, 1, rows].astype(F32)
                upright[rows] = (p_re * w_re - p_im * w_im).astype(BF16)
                upright[rows_im] = (p_re * w_im + p_im * w_re).astype(BF16)

        def forward(s, carry):
            enter(s)
            left(bigs.at[0])
            made = dot(flat[...], bigs_t[0])
            waves[s + 1, 0] = made[:, :size].astype(BF16)
            waves[s + 1, 1] = made[:, size:].astype(BF16)
            return carry
        lax.fori_loop(0, slices - 1, forward, 0)

        enter(slices - 1)
        left(bigs.at[1])
        icopy.wait()
        made = dot(flat[...], bigs_t[1])
        for e in range(4):
            rows = slice(e * 128, (e + 1) * 128)
            re, im = made[rows, :size], made[rows, size:]
            excess = re * re + im * im - intensity[rows]
            flat[rows, :size] = (excess * re).astype(BF16)
            flat[rows, size:] = (excess * im).astype(BF16)

        def backward(n, carry):
            s = slices - 1 - n
            which = jnp.where(n == 0, 1, 0)
            made = dot(flat[...], bigs[which])
            upright[:size] = made[:, :size].astype(BF16)
            upright[size:] = made[:, size:].astype(BF16)
            made = dot(bigs_t[which], upright[...])
            terms = []
            for e in range(4):
                rows = slice(e * 128, (e + 1) * 128)
                g_re, g_im = made[rows], made[size + e * 128:size + (e + 1) * 128]
                p_re, p_im = waves[s, 0, rows].astype(F32), waves[s, 1, rows].astype(F32)
                terms.append((p_re * g_re + p_im * g_im, p_re * g_im - p_im * g_re))
            for e in range(4):
                for part in range(2):
                    out[s, e, part] = jnp.where(head, terms[e][part], terms[e - 1][part]).astype(BF16)
            either(cut == s, lambda: back_copy(s).start(), lambda: back_here().start())
            for d in (2, 1, 3):
                either(cut == s if d == 2 else None,
                       lambda: block_copy(d, s).start(), lambda: block_here().start())
            for e in range(4):
                rows = slice(e * 128, (e + 1) * 128)
                g_re, g_im = made[rows], made[size + e * 128:size + (e + 1) * 128]
                w_re, w_im = window_rows(s, 0, e), window_rows(s, 1, e)
                flat[rows, :size] = (w_re * g_re + w_im * g_im).astype(BF16)
                flat[rows, size:] = (w_re * g_im - w_im * g_re).astype(BF16)
            return carry
        lax.fori_loop(0, slices, backward, 0)

    for m in range(2):
        either(is_self(2, m),
               lambda: pltpu.make_async_copy(out.at[0, 0], back.at[m], back_recv.at[m]).wait(),
               lambda: back_here().wait())
        for n in range(2):
            last_copy(m, n).start()

    for n in range(2):
        edge_copy(n).wait_send()
    for m in range(2):
        either(is_self(2, m), lambda: cross_copy(m).wait_send(), None)
        for d in (1, 2, 3):
            either(is_self(d, m), lambda: window_copy(d, m).wait_send(), None)

    @pl.when(active)
    def _():
        for k in range(4):
            either(cut == k, lambda: back_copy(k).wait_send(), None)
            for d in (1, 2, 3):
                either(cut == k if d == 2 else None,
                       lambda: block_copy(d, k).wait_send(), lambda: block_here().wait())

    for m in range(2):
        for d in range(REACH):
            either(is_self(d, m),
                   lambda: pltpu.make_async_copy(out.at[0, 0], got.at[d, m], out_recv.at[d, m]).wait(), None)
        for n in range(2):
            last_copy(m, n).wait_send()


def add_kernel(pos_ref, got, out, acc):
    width = out.shape[3]
    window = got.shape[4]
    acc[...] = jnp.zeros_like(acc)
    row = 8 * lax.broadcasted_iota(jnp.int32, (16, 8, LANES), 0) + lax.broadcasted_iota(jnp.int32, (16, 8, LANES), 1)
    lane = lax.broadcasted_iota(jnp.int32, (16, 8, LANES), 2)
    sub = lax.broadcasted_iota(jnp.int32, (17, 8, LANES), 1)
    count = window // LANES
    zero = jnp.zeros((16, 8, LANES), F32)
    gap = jnp.zeros((1, 8, LANES), F32)
    for d in range(REACH):
        for m in range(2):
            offset = lax.rem(pos_ref[d, 2 * m], 128)
            tile_row, low_row = offset // 8, lax.rem(offset, 8)
            base, shift = column_split(pos_ref[d, 2 * m + 1], width, window)
            turn = lax.rem(shift, LANES)
            mine = None
            if d == 0:
                mine = row < 128 - offset
            elif d == REACH - 1:
                mine = row >= 128 - offset
            keep = lane >= shift
            keep_row = sub >= low_row
            to_rows = pl.ds(pl.multiple_of(tile_row * 8, 8), 136)
            for part in range(2):
                before = zero
                for j in range(count + 1):
                    here = zero
                    if j < count:
                        here = got[d, m, part, :, j * LANES:(j + 1) * LANES].astype(F32).reshape(16, 8, LANES)
                        if mine is not None:
                            here = jnp.where(mine, here, 0.0)
                        here = pltpu.roll(here, turn, 2)
                    moved = pltpu.roll(jnp.where(keep, here, before), low_row, 1)
                    before = here
                    made = jnp.where(keep_row, jnp.concatenate([moved, gap]), jnp.concatenate([gap, moved]))
                    to_cols = pl.ds(pl.multiple_of(base + j * LANES, LANES), LANES)
                    acc[part, to_rows, to_cols] += made.reshape(136, LANES)
    out[:, 0] = acc[:, :128] + acc[:, 128:]


def local(probe_wave, propagator, object_slices, positions, intensities):
    count = lax.axis_size("scan")
    size = probe_wave.shape[1]
    columns = object_slices.shape[3] // LANES
    vmem = pl.BlockSpec(memory_space=pltpu.VMEM)

    def kept(x):
        return pltpu.with_memory_space_constraint(x, pltpu.HBM)

    smem = pl.BlockSpec(memory_space=pltpu.SMEM)
    anywhere = pl.BlockSpec(memory_space=pl.ANY)
    hbm = pl.BlockSpec(memory_space=pltpu.HBM)
    dma = pltpu.SemaphoreType.DMA
    pos, tiles = pl.pallas_call(
        functools.partial(positions_kernel, count),
        out_shape=[
            jax.ShapeDtypeStruct((8, LANES), jnp.int32),
            jax.ShapeDtypeStruct((2, columns, 16, 8, LANES), F32),
        ],
        in_specs=[hbm, hbm],
        out_specs=[vmem, vmem],
        scratch_shapes=[
            pltpu.SMEM((2, 2), jnp.int32), pltpu.VMEM((8, LANES), jnp.int32), pltpu.VMEM((4, 8, LANES), jnp.int32),
            dma, dma((2, columns)), dma((4,)), dma((4,))],
        compiler_params=pltpu.CompilerParams(
            collective_id=0, has_side_effects=True, vmem_limit_bytes=16 * 2**20),
        name="share_positions",
    )(kept(positions), kept(object_slices.reshape(2, 16, 8, object_slices.shape[3])))

    got = pl.pallas_call(
        functools.partial(chain_kernel, count),
        out_shape=jax.ShapeDtypeStruct((REACH, 2, 2, 128, size), BF16),
        in_specs=[smem, vmem, hbm, hbm, hbm, hbm],
        out_specs=vmem,
        scratch_shapes=[
            pltpu.VMEM((10, 2, 128, size), BF16),
            pltpu.VMEM((4, 2, size, size), BF16),
            pltpu.VMEM((size, size), F32),
            pltpu.VMEM((4, 4, 2, 128, size), BF16),
            pltpu.VMEM((2, 2, 2, 128, size), BF16),
            pltpu.VMEM((2, 2, 128, size), BF16),
            pltpu.VMEM((2, 2, 128, size), BF16),
            pltpu.VMEM((2, size, size), BF16),
            pltpu.VMEM((2, size, size), BF16),
        ]
        + [pltpu.VMEM((2, 2 * size, 2 * size), BF16)] * 2
        + [
            pltpu.VMEM((2 * size, size), BF16),
            pltpu.VMEM((size, 2 * size), BF16),
            pltpu.VMEM((4, 2, size, size), BF16),
            dma((3,)), dma((10,)), dma((4, 4)), dma, dma((2,)), dma((2,)), dma((2,)), dma,
            dma, dma, dma((4, 4)), dma((REACH, 2)), dma, dma((4,)), dma((2,)), dma, dma((2, 2)),
        ],
        compiler_params=pltpu.CompilerParams(
            collective_id=1, has_side_effects=True, vmem_limit_bytes=40 * 2**20),
        name="chain",
    )(pos, tiles, kept(intensities), kept(probe_wave), kept(propagator), kept(dft_table(size)))

    return pl.pallas_call(
        add_kernel,
        out_shape=jax.ShapeDtypeStruct(object_slices.shape, F32),
        in_specs=[smem, vmem],
        out_specs=vmem,
        scratch_shapes=[pltpu.VMEM((2, 256, object_slices.shape[3]), F32)],
        compiler_params=pltpu.CompilerParams(vmem_limit_bytes=24 * 2**20),
        name="add_gradients",
    )(pos, got)


def solution(mesh):
    in_specs = (P(), P(), P(None, "cuts", "scan", None), P("scan", None), P("scan", None, None))
    out_specs = P(None, "cuts", "scan", None)
    return jax.shard_map(local, mesh=mesh, in_specs=in_specs, out_specs=out_specs, check_vma=False)
```
